32 devices in a mesh: ctx: 4 (over x, core), exp: 8 (over z, y).
Axes of the slice: x: 2, y: 2, z: 4, core: 2. Of those that a mesh axis runs over, the one named last changes fastest.
Arguments:
- residual: bfloat16 [8, 512, 1024], P('exp', 'ctx'), may hold values from -6 to 6
- query_rows: bfloat16 [8, 512, 1024], P('exp', 'ctx'), may hold values from -8 to 8
- key_rows: bfloat16 [8, 512, 1024], P('exp', 'ctx'), may hold values from -4 to 4
- value_rows: bfloat16 [8, 512, 1024], P('exp', 'ctx'), may hold values from -6 to 6
- out_proj: bfloat16 [1024, 1024], P('exp'), may hold values from -0.75 to 0.75
- router: bfloat16 [1024, 8], replicated, may hold values from -0.5 to 0.5
- expert_ids: int32 [8, 512, 2], P('exp', 'ctx'), may hold values from 0 to 7, all different within a row; in each aligned block of 128 rows (0 to 127, 128 to 255, ..., all dimensions but the last counted through in order) at most 48 rows name the same one
- expert_gate_up: bfloat16 [8, 1024, 1536], P('exp', 'ctx'), may hold values from -0.1875 to 0.1875
- expert_down: bfloat16 [8, 768, 1024], P('exp', 'ctx'), may hold values from -0.21875 to 0.21875
Outputs:
- layer_out: bfloat16 [8, 512, 1024], P('exp', 'ctx')
The draws below stay inside these ranges and needn't reach their ends.
Inputs may be any that keep to these rules, and one draw needn't show every extreme that they name: `expert_ids`: the 2 ids of a token differ. Among the 128 tokens of one device (aligned blocks of 128 tokens of the flattened sequences) each expert is named at most 48 times, a bound that some block reaches.
All inputs are finite; a program needn't handle non-finite values.
Results may differ from the reference program's by a relative error of at most 0.017.
Values may be sent and summed in bfloat16 or wider, within the bound.
A program may use at most 64 MiB of HBM per device.

```python
import math
import jax
import jax.numpy as jnp
import numpy as np
from jax import lax

D = 1024
HEADS = 8
HEAD_DIM = 128
FF = 768
TOP = 2
TOK_DEV = 128
HD = 1024
SEQ_LEN = 512
SEQS = 8
EXPERTS = 8
CAP = 48
N_CTX = 4
N_EXP = 8


def draw_query_rows(key, part):
    sample = 2.0 * jnp.clip(jax.random.normal(jax.random.fold_in(key, 1), (SEQS, SEQ_LEN, HD), jnp.float32), -4.0, 4.0)
    return sample.astype(jnp.bfloat16)


def draw_key_rows(key, part):
    sample = jnp.clip(jax.random.normal(jax.random.fold_in(key, 2), (SEQS, SEQ_LEN, HD), jnp.float32), -4.0, 4.0)
    return sample.astype(jnp.bfloat16)


def block_scale(stream_key, shape, split, smallest, largest):
    loudness = 1.0
    for dim, blocks in split:
        heights = jax.random.uniform(jax.random.fold_in(jax.random.fold_in(stream_key, 6), dim), (blocks,), jnp.float32, smallest / len(split), largest / len(split))
        loudness = loudness * jnp.repeat(jnp.exp(heights), shape[dim] // blocks).reshape((-1,) + (1,) * (len(shape) - 1 - dim))
    return loudness


def routed_block(own_key, own, number, rows, count, top, bound, skew):
    order = jax.random.permutation(own_key, count)
    packed, ordinary = portions_of(count, rows * top, bound, skew, True), portions_of(count, rows * top, bound, skew, False)
    places = jnp.arange(count)

    def named(sizes, turn):
        used = int((sizes > 0).sum())
        fixed = max(1, used // 4)
        passed = fixed + (places - fixed + turn * (used - fixed)) % max(1, count - fixed)
        return jnp.zeros((count,), jnp.int32).at[order[jnp.where(places < fixed, places, passed)]].set(jnp.asarray(sizes, jnp.int32))

    sizes = jnp.where(number % 4 == 0, named(packed, number // 4), named(ordinary, number - number // 4 - 1))
    mixed = jax.random.permutation(jax.random.fold_in(own, 3), count)
    source_of, receiver = mixed[0:count // 2 * 2:2], mixed[1:count // 2 * 2:2]
    room = jnp.minimum(sizes[source_of] - 1, bound - sizes[receiver]) // 2
    room = jnp.where((source_of == order[0]) | (receiver == order[0]) | (sizes[receiver] == 0), 0, jnp.maximum(room, 0))
    passed = jax.random.randint(jax.random.fold_in(own, 4), (count // 2,), 0, 1 << 20) % (room + 1)
    sizes = sizes.at[source_of].add(-passed).at[receiver].add(passed)
    items = jnp.searchsorted(jnp.cumsum(sizes), jnp.arange(rows * top), side="right").astype(jnp.int32)
    listing = items.reshape(top, rows).T
    listing = listing[jax.random.permutation(jax.random.fold_in(own, 1), rows)]
    turn = jax.random.randint(jax.random.fold_in(own, 2), (rows, 1), 0, top)
    return jnp.take_along_axis(listing, (jnp.arange(top)[None, :] + turn) % top, axis=1)


def portions_of(count, total, reach, skew, full):
    loads = [(1 << 20) // math.isqrt(rank ** skew) + 1 for rank in range(1, count + 1)]
    largest = reach if full else min(reach, max(-(-total // count), total * loads[0] // sum(loads)))
    least = 1 if total - largest >= count - 1 else 0
    counts, surplus = [largest] + [least] * (count - 1), total - largest - least * (count - 1)
    while surplus > 0:
        free = [i for i in range(1, count) if counts[i] < largest] or [i for i in range(1, count) if counts[i] < reach]
        pool, budget = sum([loads[i] for i in free]), surplus
        for i in free:
            addition = min(reach - counts[i], max(1, budget * loads[i] // pool), surplus)
            counts[i] = counts[i] + addition
            surplus = surplus - addition
    return np.array(counts)


def bell_draw(rng, shape, spread, bound, cuts=(), held_as=jnp.bfloat16):
    entries = jax.random.normal(rng, shape, jnp.float32) * spread
    if len(cuts) > 0:
        entries = block_scale(rng, shape, cuts, -0.22, 0.18) * entries
    return jnp.clip(entries, min=-bound, max=bound).astype(held_as)


def setup_inputs(seed: int = 0) -> dict:
    seeds = jax.random.split(jax.random.key(seed), 10)
    residual = bell_draw(seeds[0], (SEQS, SEQ_LEN, D), 1.0, 6.0, ((0, 8), (1, 4)))
    query_rows = draw_query_rows(jax.random.fold_in(seeds[9], 71), 0)
    key_rows = draw_key_rows(jax.random.fold_in(seeds[9], 71), 0)
    value_rows = bell_draw(seeds[3], (SEQS, SEQ_LEN, HD), 1.0, 6.0, ((0, 8), (1, 4)))
    out_proj = bell_draw(seeds[4], (HD, D), (HD // 16) ** -0.5, 0.75, ((0, 8),))
    router = bell_draw(seeds[5], (D, EXPERTS), (D // 9) ** -0.5, 0.5)
    expert_ids_keys = jax.random.split(jax.random.fold_in(seeds[6], 1), SEQS * SEQ_LEN // TOK_DEV)
    expert_ids_turns = jax.random.permutation(jax.random.fold_in(seeds[6], 3), SEQS * SEQ_LEN // TOK_DEV)
    expert_ids = jax.vmap(lambda own, number: routed_block(jax.random.fold_in(seeds[6], 2), own, number, TOK_DEV, EXPERTS, TOP, CAP, 2))(expert_ids_keys, expert_ids_turns).reshape((SEQS, SEQ_LEN, TOP))
    expert_gate_up = bell_draw(seeds[7], (EXPERTS, D, 2 * FF), D ** -0.5, 0.1875, ((0, 8), (1, 4)))
    expert_down = bell_draw(seeds[8], (EXPERTS, FF, D), FF ** -0.5, 0.21875, ((0, 8), (1, 4)))
    return dict(residual=residual, query_rows=query_rows, key_rows=key_rows, value_rows=value_rows, out_proj=out_proj, router=router, expert_ids=expert_ids, expert_gate_up=expert_gate_up, expert_down=expert_down)


NEG_FILL = -1e+30

def attend_sequence(operands):
    query_seq, key_seq, value_seq = operands
    length = query_seq.shape[0]
    scale_factor = HEAD_DIM ** (-0.5)
    query_heads = query_seq.astype(jnp.float32).reshape(length, HEADS, HEAD_DIM).transpose(1, 0, 2)
    key_heads = key_seq.astype(jnp.float32).reshape(length, HEADS, HEAD_DIM).transpose(1, 0, 2)
    value_heads = value_seq.astype(jnp.float32).reshape(length, HEADS, HEAD_DIM).transpose(1, 0, 2)
    position = jnp.arange(length)
    allowed = position[None, :] <= position[:, None]

    def one_head(head_operands):
        query_head, key_head, value_head = head_operands
        scores = jnp.dot(query_head, key_head.T, preferred_element_type=jnp.float32) * scale_factor
        row_max = lax.optimization_barrier(jnp.max(jnp.where(allowed, scores, NEG_FILL), axis=1, keepdims=True))
        exp_scores = jnp.where(allowed, jnp.exp(scores - row_max), 0.0)
        denominator = lax.optimization_barrier(jnp.sum(exp_scores, axis=1, keepdims=True))
        prob_bf = lax.optimization_barrier(exp_scores.astype(jnp.bfloat16)).astype(jnp.float32)
        return jnp.dot(prob_bf, value_head, preferred_element_type=jnp.float32) / denominator
    per_head = lax.map(one_head, (query_heads, key_heads, value_heads))
    return per_head.transpose(1, 0, 2).reshape(length, HEADS * HEAD_DIM).astype(jnp.bfloat16)

def reference(residual, query_rows, key_rows, value_rows, out_proj, router, expert_ids, expert_gate_up, expert_down):
    context = lax.map(attend_sequence, (query_rows, key_rows, value_rows))
    token_total = SEQS * SEQ_LEN
    attn_out = jnp.dot(context.reshape(token_total, HEADS * HEAD_DIM), out_proj, preferred_element_type=jnp.float32)
    hidden_state = (residual.reshape(token_total, D).astype(jnp.float32) + attn_out).astype(jnp.bfloat16)
    hidden_wide = hidden_state.astype(jnp.float32)
    mean_square = lax.optimization_barrier(jnp.mean(hidden_wide * hidden_wide, axis=1, keepdims=True))
    normed = (hidden_wide * lax.rsqrt(mean_square + 1e-06)).astype(jnp.bfloat16)
    affinity = jax.nn.sigmoid(jnp.dot(normed, router, preferred_element_type=jnp.float32))
    chosen_ids = expert_ids.reshape(token_total, TOP).astype(jnp.int32)
    picked = jnp.take_along_axis(affinity, chosen_ids, axis=1)
    gate_share = picked / lax.optimization_barrier(jnp.sum(picked, axis=1, keepdims=True))
    pair_ids = chosen_ids.reshape(token_total * TOP)
    slot_bound = N_EXP * N_CTX * CAP

    def one_expert(expert, collected):
        members = jnp.nonzero(pair_ids == expert, size=slot_bound, fill_value=token_total * TOP)[0].astype(jnp.int32)
        token_index = jnp.minimum(members // TOP, token_total - 1).astype(jnp.int32)
        token_feats = jnp.take(normed, token_index, axis=0)
        gate_up_out = jnp.dot(token_feats, expert_gate_up[expert], preferred_element_type=jnp.float32)
        activation = (jax.nn.silu(gate_up_out[:, :FF]) * gate_up_out[:, FF:]).astype(jnp.bfloat16)
        produced = jnp.dot(activation, expert_down[expert], preferred_element_type=jnp.float32).astype(jnp.bfloat16)
        return collected.at[members].set(produced, mode='drop')
    collected = lax.fori_loop(0, EXPERTS, one_expert, jnp.zeros((token_total * TOP, D), jnp.bfloat16))
    pair_out = collected.reshape(token_total, TOP, D).astype(jnp.float32)
    moe_out = lax.optimization_barrier(jnp.sum(gate_share[:, :, None] * pair_out, axis=1))
    return (hidden_wide + moe_out).astype(jnp.bfloat16).reshape(SEQS, SEQ_LEN, D)
```

```python
import functools

import jax
import jax.numpy as jnp
from jax import lax
from jax.experimental import pallas as pl
from jax.experimental.pallas import tpu as pltpu
from jax.sharding import PartitionSpec as P

HEADS = 8
HEAD_DIM = 128
NEG_FILL = -1e30
MESH = pl.DeviceIdType.MESH


def fused(
    n_ctx,
    n_exp,
    cap,
    residual,
    query,
    router,
    ids_ref,
    key,
    value,
    out_proj,
    gate_up,
    down,
    out,
    kbuf,
    vbuf,
    proj,
    gbuf,
    dbuf,
    outgoing,
    arrived,
    produced,
    returned,
    context,
    activation,
    local_sem,
    k_send,
    k_recv,
    v_send,
    v_recv,
    g_send,
    g_recv,
    d_send,
    d_recv,
    proj_send,
    proj_recv,
    proj_fwd,
    out_send,
    out_recv,
    back_send,
    back_recv,
):
    chips = n_ctx // 2
    c = lax.axis_index("ctx")
    e = lax.axis_index("exp")
    chip = c // 2
    core = lax.rem(c, 2)
    sibling = chip * 2 + 1 - core
    tok = query.shape[1]
    width = query.shape[2]
    half = out_proj.shape[0] // 2

    def chip_at(r):
        return lax.rem(chip + r, chips) * 2 + core

    def exp_at(r):
        return lax.rem(e + r, n_exp)

    barrier = pltpu.get_barrier_semaphore()
    for r in range(1, n_exp):
        pl.semaphore_signal(barrier, inc=1, device_id={"exp": exp_at(r)}, device_id_type=MESH)
    for r in range(1, chips):
        pl.semaphore_signal(barrier, inc=1, device_id={"ctx": chip_at(r)}, device_id_type=MESH)
    pl.semaphore_signal(barrier, inc=1, device_id={"ctx": sibling}, device_id_type=MESH)

    locals_ = [
        pltpu.make_async_copy(key.at[0], kbuf.at[c], local_sem.at[0]),
        pltpu.make_async_copy(value.at[0], vbuf.at[c], local_sem.at[1]),
        pltpu.make_async_copy(out_proj.at[pl.ds(0, half)], proj.at[e, 0], local_sem.at[2]),
        pltpu.make_async_copy(out_proj.at[pl.ds(half, half)], proj.at[e, 1], local_sem.at[3]),
        pltpu.make_async_copy(gate_up.at[0], gbuf.at[c], local_sem.at[4]),
        pltpu.make_async_copy(down.at[0], dbuf.at[c], local_sem.at[5]),
    ]
    for copy in locals_:
        copy.start()
    pl.semaphore_wait(barrier, n_exp - 1 + chips - 1 + 1)

    pending = []

    def remote(src, dst, send, recv, where):
        return pltpu.make_async_remote_copy(
            src_ref=src, dst_ref=dst, send_sem=send, recv_sem=recv, device_id=where, device_id_type=MESH
        )

    def spread(src, buf, send, recv):
        copies = []
        for r in range(1, chips):
            copies.append(remote(src, buf.at[c], send.at[r - 1], recv.at[c], {"ctx": chip_at(r)}))
        copies.append(remote(src, buf.at[c], send.at[chips - 1], recv.at[c], {"ctx": sibling}))
        for copy in copies:
            copy.start()
        return copies

    def landed(buf, send, recv, s):
        remote(buf.at[s], buf.at[s], send.at[0], recv.at[s], {"ctx": sibling}).wait_recv()

    def forward(buf, send, recv):
        for r in range(1, chips):
            s = chip_at(chips - r)
            landed(buf, send, recv, s)
            copy = remote(buf.at[s], buf.at[s], send.at[chips - 1 + r], recv.at[s], {"ctx": sibling})
            copy.start()
            pending.append(copy)

    def from_sibling(buf, send, recv):
        for r in range(chips):
            landed(buf, send, recv, lax.rem(chip + r, chips) * 2 + 1 - core)

    k_copies = spread(key.at[0], kbuf, k_send, k_recv)
    v_copies = spread(value.at[0], vbuf, v_send, v_recv)
    offsets = [0]
    for r in range(1, n_exp // 2 + 1):
        offsets.append(r)
        if n_exp - r != r:
            offsets.append(n_exp - r)
    own_half = out_proj.at[pl.ds(pl.multiple_of(core * half, half), half)]
    for r in reversed(offsets[1:]):
        copy = remote(own_half, proj.at[e, core], proj_send.at[r], proj_recv.at[e, core], {"exp": exp_at(r)})
        copy.start()
        pending.append(copy)

    forward(kbuf, k_send, k_recv)
    forward(vbuf, v_send, v_recv)
    for copy in k_copies + v_copies:
        copy.wait_send()
    pending.extend(spread(gate_up.at[0], gbuf, g_send, g_recv))
    pending.extend(spread(down.at[0], dbuf, d_send, d_recv))

    def proj_at(s, side):
        return remote(proj.at[s, side], proj.at[s, side], proj_fwd.at[s], proj_recv.at[s, side], {"ctx": sibling})

    for r in offsets[1:]:
        s = exp_at(r)
        proj_at(s, core).wait_recv()
        copy = proj_at(s, core)
        copy.start()
        pending.append(copy)

    for copy in locals_:
        copy.wait()
    from_sibling(kbuf, k_send, k_recv)
    from_sibling(vbuf, v_send, v_recv)

    keys = n_ctx * tok
    q_pos = c * tok + lax.broadcasted_iota(jnp.int32, (tok, keys), 0)
    k_pos = lax.broadcasted_iota(jnp.int32, (tok, keys), 1)
    allowed = k_pos <= q_pos
    for h in range(HEADS):
        cols = slice(h * HEAD_DIM, (h + 1) * HEAD_DIM)
        k_head = kbuf[:, :, cols].reshape(keys, HEAD_DIM)
        v_head = vbuf[:, :, cols].reshape(keys, HEAD_DIM)
        scores = lax.dot_general(
            query[0, :, cols], k_head, (((1,), (1,)), ((), ())), preferred_element_type=jnp.float32
        )
        scores = jnp.where(allowed, scores * (HEAD_DIM**-0.5), NEG_FILL)
        weights = jnp.exp(scores - jnp.max(scores, axis=1, keepdims=True))
        total = jnp.sum(weights, axis=1, keepdims=True)
        part = jnp.dot(weights.astype(jnp.bfloat16), v_head, preferred_element_type=jnp.float32)
        context[:, cols] = (part / total).astype(jnp.bfloat16)

    for r in offsets[1:]:
        proj_at(exp_at(r), 1 - core).wait_recv()
    attn_out = jnp.dot(
        context[...], proj[...].reshape(n_exp * 2 * half, width), preferred_element_type=jnp.float32
    )
    hidden = (residual[0].astype(jnp.float32) + attn_out).astype(jnp.bfloat16)
    wide = hidden.astype(jnp.float32)
    mean_square = jnp.mean(wide * wide, axis=1, keepdims=True)
    normed = (wide * lax.rsqrt(mean_square + 1e-06)).astype(jnp.bfloat16)

    ids = ids_ref[0]
    slots = []
    for k in range(2):
        away = ids[:, k : k + 1] - e
        away = jnp.where(away < 0, away + n_exp, away)
        slot = jnp.where(2 * away <= n_exp, 2 * away - 1, 2 * (n_exp - away))
        slots.append(jnp.where(away == 0, 0, slot))
    lane = lax.broadcasted_iota(jnp.int32, (tok, 128), 1)
    picks = [lane == slots[k] for k in range(2)]
    member = jnp.where(picks[0] | picks[1], 1.0, 0.0)
    below = jnp.where(
        lax.broadcasted_iota(jnp.int32, (tok, tok), 1) < lax.broadcasted_iota(jnp.int32, (tok, tok), 0), 1.0, 0.0
    ).astype(jnp.bfloat16)
    rank = jnp.dot(below, member.astype(jnp.bfloat16), preferred_element_type=jnp.float32)
    place = (member * (rank + 1.0)).astype(jnp.bfloat16)
    grid = (n_exp, cap, 128)
    rows = n_exp * cap
    spread_out = jnp.where(
        lax.broadcasted_iota(jnp.int32, grid, 0) == lax.broadcasted_iota(jnp.int32, grid, 2), 1.0, 0.0
    ).reshape(rows, 128)
    wanted = (lax.broadcasted_iota(jnp.int32, (n_exp, cap, tok), 1) + 1).astype(jnp.float32).reshape(rows, tok)
    held = lax.dot_general(
        spread_out.astype(jnp.bfloat16), place, (((1,), (1,)), ((), ())), preferred_element_type=jnp.float32
    )
    dispatch = jnp.where(held == wanted, 1.0, 0.0).astype(jnp.bfloat16)
    sent = jnp.dot(dispatch, normed, preferred_element_type=jnp.float32).astype(jnp.bfloat16)
    outgoing[...] = sent.reshape(n_exp, cap, width)
    for i in reversed(range(1, n_exp)):
        copy = remote(
            outgoing.at[i], arrived.at[i], out_send.at[i], out_recv.at[i], {"exp": exp_at(offsets[i])}
        )
        copy.start()
        pending.append(copy)
    arrived[0] = outgoing[0]

    affinity = jax.nn.sigmoid(jnp.dot(normed, router[...], preferred_element_type=jnp.float32))
    expert_lane = lax.broadcasted_iota(jnp.int32, affinity.shape, 1)
    picked = [
        jnp.sum(jnp.where(expert_lane == ids[:, k : k + 1], affinity, 0.0), axis=1, keepdims=True) for k in range(2)
    ]
    both = picked[0] + picked[1]
    column = lax.broadcasted_iota(jnp.int32, (tok, rows), 1).astype(jnp.float32)
    combine = jnp.zeros((tok, rows), jnp.float32)
    for k in range(2):
        own_rank = jnp.sum(jnp.where(picks[k], rank, 0.0), axis=1, keepdims=True)
        target = slots[k].astype(jnp.float32) * cap + own_rank
        combine = combine + jnp.where(column == target, picked[k] / both, 0.0)
    combine = combine.astype(jnp.bfloat16)

    forward(gbuf, g_send, g_recv)
    forward(dbuf, d_send, d_recv)
    from_sibling(gbuf, g_send, g_recv)
    from_sibling(dbuf, d_send, d_recv)

    ff = activation.shape[1]
    group = n_exp // 2
    chunk = 256
    for first in range(0, n_exp, group):
        for i in range(max(first, 1), first + group):
            remote(outgoing.at[i], arrived.at[i], out_send.at[i], out_recv.at[i], {"exp": exp_at(offsets[i])}).wait_recv()
        feats = arrived[first : first + group].reshape(group * cap, width)
        for f in range(0, ff, chunk):
            gate = jnp.dot(
                feats, gbuf[:, :, f : f + chunk].reshape(width, chunk), preferred_element_type=jnp.float32
            )
            up = jnp.dot(
                feats, gbuf[:, :, ff + f : ff + f + chunk].reshape(width, chunk), preferred_element_type=jnp.float32
            )
            activation[:, f : f + chunk] = (gate / (1.0 + jnp.exp(-gate)) * up).astype(jnp.bfloat16)
        made = jnp.dot(activation[...], dbuf[...].reshape(ff, width), preferred_element_type=jnp.float32)
        produced[first : first + group] = made.astype(jnp.bfloat16).reshape(group, cap, width)
        for i in reversed(range(max(first, 1), first + group)):
            copy = remote(
                produced.at[i],
                returned.at[i],
                back_send.at[i],
                back_recv.at[i],
                {"exp": exp_at(n_exp - offsets[i])},
            )
            copy.start()
            pending.append(copy)
    returned[0] = produced[0]
    for i in range(1, n_exp):
        remote(produced.at[i], returned.at[i], back_send.at[i], back_recv.at[i], {"exp": exp_at(offsets[i])}).wait_recv()
    moe = jnp.dot(combine, returned[...].reshape(rows, width), preferred_element_type=jnp.float32)
    out[0] = (wide + moe).astype(jnp.bfloat16)
    for copy in pending:
        copy.wait_send()


def on_device(
    residual, query_rows, key_rows, value_rows, out_proj, router, expert_ids, expert_gate_up, expert_down
):
    n_ctx = lax.axis_size("ctx")
    n_exp = lax.axis_size("exp")
    chips = n_ctx // 2
    _, tok, width = residual.shape
    cap = min(tok, -(-(3 * tok // n_exp) // 16) * 16)
    bf16 = jnp.bfloat16
    depth, twice_ff = expert_gate_up.shape[1:]
    ff_part = expert_down.shape[1]
    half = out_proj.shape[0] // 2
    vmem = pl.BlockSpec(memory_space=pltpu.VMEM)
    anywhere = pl.BlockSpec(memory_space=pl.ANY)
    dma = pltpu.SemaphoreType.DMA
    ctx_sems = [dma((2 * chips,)), dma((n_ctx,))]
    rows = n_exp * cap
    return pl.pallas_call(
        functools.partial(fused, n_ctx, n_exp, cap),
        out_shape=jax.ShapeDtypeStruct(residual.shape, bf16),
        in_specs=[vmem] * 4 + [anywhere] * 5,
        out_specs=vmem,
        scratch_shapes=[
            pltpu.VMEM((n_ctx, tok, width), bf16),
            pltpu.VMEM((n_ctx, tok, width), bf16),
            pltpu.VMEM((n_exp, 2, half, width), bf16),
            pltpu.VMEM((n_ctx, depth, twice_ff), bf16),
            pltpu.VMEM((n_ctx, ff_part, width), bf16),
            pltpu.VMEM((n_exp, cap, width), bf16),
            pltpu.VMEM((n_exp, cap, width), bf16),
            pltpu.VMEM((n_exp, cap, width), bf16),
            pltpu.VMEM((n_exp, cap, width), bf16),
            pltpu.VMEM((tok, width), bf16),
            pltpu.VMEM((rows // 2, twice_ff // 2), bf16),
            dma((6,)),
        ]
        + ctx_sems * 4
        + [dma((n_exp,)), dma((n_exp, 2)), dma((n_exp,))]
        + [dma((n_exp,))] * 4,
        compiler_params=pltpu.CompilerParams(
            collective_id=0, has_side_effects=True, vmem_limit_bytes=48 * 1024 * 1024
        ),
    )(residual, query_rows, router, expert_ids, key_rows, value_rows, out_proj, expert_gate_up, expert_down)


def solution(mesh):
    return jax.shard_map(
        on_device,
        mesh=mesh,
        in_specs=(
            P("exp", "ctx", None),
            P("exp", "ctx", None),
            P("exp", "ctx", None),
            P("exp", "ctx", None),
            P("exp", None),
            P(),
            P("exp", "ctx", None),
            P("exp", "ctx", None),
            P("exp", "ctx", None),
        ),
        out_specs=P("exp", "ctx", None),
        check_vma=False,
    )
```

```python
import functools

import jax
import jax.numpy as jnp
from jax import lax
from jax.experimental import pallas as pl
from jax.experimental.pallas import tpu as pltpu
from jax.sharding import PartitionSpec as P

HEADS = 8
HEAD_DIM = 128
NEG_FILL = -1e30
MESH = pl.DeviceIdType.MESH


def fused(
    n_ctx,
    n_exp,
    cap,
    residual_in,
    query_in,
    router_in,
    ids_in,
    key,
    value,
    out_proj,
    gate_up,
    down,
    out,
    residual,
    query,
    router,
    ids_ref,
    kvbuf,
    proj,
    gbuf,
    dbuf,
    outgoing,
    arrived,
    produced,
    returned,
    context,
    activation,
    local_sem,
    kv_local,
    kv_send,
    kv_recv,
    g_send,
    g_recv,
    d_send,
    d_recv,
    proj_send,
    proj_recv,
    proj_fwd,
    out_send,
    out_recv,
    back_send,
    back_recv,
):
    chips = n_ctx // 2
    c = lax.axis_index("ctx")
    e = lax.axis_index("exp")
    chip = c // 2
    core = lax.rem(c, 2)
    sibling = chip * 2 + 1 - core
    tok, width = query.shape
    groups = kvbuf.shape[1] // 2
    group_cols = kvbuf.shape[3]
    half = out_proj.shape[0] // 2

    def chip_at(r):
        return lax.rem(chip + r, chips) * 2 + core

    def exp_at(r):
        return lax.rem(e + r, n_exp)

    barrier = pltpu.get_barrier_semaphore()
    for r in range(1, n_exp):
        pl.semaphore_signal(barrier, inc=1, device_id={"exp": exp_at(r)}, device_id_type=MESH)
    for r in range(1, chips):
        pl.semaphore_signal(barrier, inc=1, device_id={"ctx": chip_at(r)}, device_id_type=MESH)
    pl.semaphore_signal(barrier, inc=1, device_id={"ctx": sibling}, device_id_type=MESH)

    locals_ = [
        pltpu.make_async_copy(query_in.at[0], query, local_sem.at[0]),
        pltpu.make_async_copy(residual_in.at[0], residual, local_sem.at[1]),
        pltpu.make_async_copy(out_proj.at[pl.ds(0, half)], proj.at[e, 0], local_sem.at[2]),
        pltpu.make_async_copy(out_proj.at[pl.ds(half, half)], proj.at[e, 1], local_sem.at[3]),
        pltpu.make_async_copy(gate_up.at[0], gbuf.at[c], local_sem.at[4]),
        pltpu.make_async_copy(down.at[0], dbuf.at[c], local_sem.at[5]),
        pltpu.make_async_copy(router_in, router, local_sem.at[6]),
        pltpu.make_async_copy(ids_in.at[0], ids_ref, local_sem.at[7]),
    ]
    kv_parts = []
    for g in range(groups):
        for ref in (key, value):
            kv_parts.append(ref.at[0, :, pl.ds(g * group_cols, group_cols)])
    for i, part in enumerate(kv_parts):
        locals_.append(pltpu.make_async_copy(part, kvbuf.at[c, i], kv_local.at[i]))
    for copy in locals_:
        copy.start()
    pl.semaphore_wait(barrier, n_exp - 1 + chips - 1 + 1)

    pending = []

    def remote(src, dst, send, recv, where):
        return pltpu.make_async_remote_copy(
            src_ref=src, dst_ref=dst, send_sem=send, recv_sem=recv, device_id=where, device_id_type=MESH
        )

    def spread(src, buf, send, recv):
        copies = []
        for r in range(1, chips):
            copies.append(remote(src, buf.at[c], send.at[r - 1], recv.at[c], {"ctx": chip_at(r)}))
        copies.append(remote(src, buf.at[c], send.at[chips - 1], recv.at[c], {"ctx": sibling}))
        for copy in copies:
            copy.start()
        return copies

    def landed(buf, send, recv, s):
        remote(buf.at[s], buf.at[s], send.at[0], recv.at[s], {"ctx": sibling}).wait_recv()

    def forward(buf, send, recv):
        for r in range(1, chips):
            s = chip_at(chips - r)
            landed(buf, send, recv, s)
            copy = remote(buf.at[s], buf.at[s], send.at[chips - 1 + r], recv.at[s], {"ctx": sibling})
            copy.start()
            pending.append(copy)

    def from_sibling(buf, send, recv):
        for r in range(chips):
            landed(buf, send, recv, lax.rem(chip + r, chips) * 2 + 1 - core)

    kv_copies = []
    kv_views = [(kvbuf.at[:, i], kv_send.at[i], kv_recv.at[i]) for i in range(2 * groups)]
    for part, view in zip(kv_parts, kv_views):
        kv_copies += spread(part, *view)
    offsets = [0]
    for r in range(1, n_exp // 2 + 1):
        offsets.append(r)
        if n_exp - r != r:
            offsets.append(n_exp - r)
    own_half = out_proj.at[pl.ds(pl.multiple_of(core * half, half), half)]
    for r in reversed(offsets[1:]):
        copy = remote(own_half, proj.at[e, core], proj_send.at[r], proj_recv.at[e, core], {"exp": exp_at(r)})
        copy.start()
        pending.append(copy)

    def proj_at(s, side):
        return remote(proj.at[s, side], proj.at[s, side], proj_fwd.at[s], proj_recv.at[s, side], {"ctx": sibling})

    for copy in locals_:
        copy.wait()
    keys = n_ctx * tok
    q_pos = c * tok + lax.broadcasted_iota(jnp.int32, (tok, keys), 0)
    k_pos = lax.broadcasted_iota(jnp.int32, (tok, keys), 1)
    allowed = k_pos <= q_pos
    for g in range(groups):
        forward(*kv_views[2 * g])
        forward(*kv_views[2 * g + 1])
        if g == groups - 1:
            for copy in kv_copies:
                copy.wait_send()
            pending.extend(spread(gate_up.at[0], gbuf, g_send, g_recv))
            pending.extend(spread(down.at[0], dbuf, d_send, d_recv))
            for r in offsets[1:]:
                s = exp_at(r)
                proj_at(s, core).wait_recv()
                copy = proj_at(s, core)
                copy.start()
                pending.append(copy)
        from_sibling(*kv_views[2 * g])
        from_sibling(*kv_views[2 * g + 1])
        for h in range(group_cols // HEAD_DIM):
            inner = slice(h * HEAD_DIM, (h + 1) * HEAD_DIM)
            cols = slice(g * group_cols + h * HEAD_DIM, g * group_cols + (h + 1) * HEAD_DIM)
            k_head = kvbuf[:, 2 * g, :, inner].reshape(keys, HEAD_DIM)
            v_head = kvbuf[:, 2 * g + 1, :, inner].reshape(keys, HEAD_DIM)
            scores = lax.dot_general(
                query[:, cols], k_head, (((1,), (1,)), ((), ())), preferred_element_type=jnp.float32
            )
            scores = jnp.where(allowed, scores * (HEAD_DIM**-0.5), NEG_FILL)
            weights = jnp.exp(scores - jnp.max(scores, axis=1, keepdims=True))
            total = jnp.sum(weights, axis=1, keepdims=True)
            part = jnp.dot(weights.astype(jnp.bfloat16), v_head, preferred_element_type=jnp.float32)
            context[:, cols] = (part / total).astype(jnp.bfloat16)

    for r in offsets[1:]:
        proj_at(exp_at(r), 1 - core).wait_recv()
    attn_out = jnp.dot(
        context[...], proj[...].reshape(n_exp * 2 * half, width), preferred_element_type=jnp.float32
    )
    hidden = (residual[...].astype(jnp.float32) + attn_out).astype(jnp.bfloat16)
    wide = hidden.astype(jnp.float32)
    mean_square = jnp.mean(wide * wide, axis=1, keepdims=True)
    normed = (wide * lax.rsqrt(mean_square + 1e-06)).astype(jnp.bfloat16)

    eye = jnp.where(
        lax.broadcasted_iota(jnp.int32, (tok, tok), 1) == lax.broadcasted_iota(jnp.int32, (tok, tok), 0), 1.0, 0.0
    ).astype(jnp.bfloat16)
    ids = lax.dot_general(
        eye,
        ids_ref[...].astype(jnp.float32).astype(jnp.bfloat16),
        (((1,), (1,)), ((), ())),
        preferred_element_type=jnp.float32,
    ).astype(jnp.int32)
    slots = []
    for k in range(2):
        away = ids[:, k : k + 1] - e
        away = jnp.where(away < 0, away + n_exp, away)
        slot = jnp.where(2 * away <= n_exp, 2 * away - 1, 2 * (n_exp - away))
        slots.append(jnp.where(away == 0, 0, slot))
    lane = lax.broadcasted_iota(jnp.int32, (tok, 128), 1)
    picks = [lane == slots[k] for k in range(2)]
    member = jnp.where(picks[0] | picks[1], 1.0, 0.0)
    below = jnp.where(
        lax.broadcasted_iota(jnp.int32, (tok, tok), 1) < lax.broadcasted_iota(jnp.int32, (tok, tok), 0), 1.0, 0.0
    ).astype(jnp.bfloat16)
    rank = jnp.dot(below, member.astype(jnp.bfloat16), preferred_element_type=jnp.float32)
    place = (member * (rank + 1.0)).astype(jnp.bfloat16)
    grid = (n_exp, cap, 128)
    rows = n_exp * cap
    spread_out = jnp.where(
        lax.broadcasted_iota(jnp.int32, grid, 0) == lax.broadcasted_iota(jnp.int32, grid, 2), 1.0, 0.0
    ).reshape(rows, 128)
    wanted = (lax.broadcasted_iota(jnp.int32, (n_exp, cap, tok), 1) + 1).astype(jnp.float32).reshape(rows, tok)
    held = lax.dot_general(
        spread_out.astype(jnp.bfloat16), place, (((1,), (1,)), ((), ())), preferred_element_type=jnp.float32
    )
    dispatch = jnp.where(held == wanted, 1.0, 0.0).astype(jnp.bfloat16)
    sent = jnp.dot(dispatch, normed, preferred_element_type=jnp.float32).astype(jnp.bfloat16)
    outgoing[...] = sent.reshape(n_exp, cap, width)
    for i in reversed(range(1, n_exp)):
        copy = remote(
            outgoing.at[i], arrived.at[i], out_send.at[i], out_recv.at[i], {"exp": exp_at(offsets[i])}
        )
        copy.start()
        pending.append(copy)
    arrived[0] = outgoing[0]

    affinity = jax.nn.sigmoid(
        lax.dot_general(normed, router[...], (((1,), (1,)), ((), ())), preferred_element_type=jnp.float32)
    )
    expert_lane = lax.broadcasted_iota(jnp.int32, affinity.shape, 1)
    picked = [
        jnp.sum(jnp.where(expert_lane == ids[:, k : k + 1], affinity, 0.0), axis=1, keepdims=True) for k in range(2)
    ]
    both = picked[0] + picked[1]
    column = lax.broadcasted_iota(jnp.int32, (tok, rows), 1).astype(jnp.float32)
    combine = jnp.zeros((tok, rows), jnp.float32)
    for k in range(2):
        own_rank = jnp.sum(jnp.where(picks[k], rank, 0.0), axis=1, keepdims=True)
        target = slots[k].astype(jnp.float32) * cap + own_rank
        combine = combine + jnp.where(column == target, picked[k] / both, 0.0)
    combine = combine.astype(jnp.bfloat16)

    forward(gbuf, g_send, g_recv)
    from_sibling(gbuf, g_send, g_recv)
    ff = activation.shape[1]
    group = n_exp // 2
    chunk = 256
    for first in range(0, n_exp, group):
        for i in range(max(first, 1), first + group):
            remote(
                outgoing.at[i], arrived.at[i], out_send.at[i], out_recv.at[i], {"exp": exp_at(offsets[i])}
            ).wait_recv()
        feats = arrived[first : first + group].reshape(group * cap, width)
        for f in range(0, ff, chunk):
            gate = jnp.dot(
                feats, gbuf[:, :, f : f + chunk].reshape(width, chunk), preferred_element_type=jnp.float32
            )
            up = jnp.dot(
                feats, gbuf[:, :, ff + f : ff + f + chunk].reshape(width, chunk), preferred_element_type=jnp.float32
            )
            activation[first * cap : (first + group) * cap, f : f + chunk] = (
                gate / (1.0 + jnp.exp(-gate)) * up
            ).astype(jnp.bfloat16)
    forward(dbuf, d_send, d_recv)
    from_sibling(dbuf, d_send, d_recv)
    for first in (group, 0):
        made = jnp.dot(
            activation[first * cap : (first + group) * cap],
            dbuf[...].reshape(ff, width),
            preferred_element_type=jnp.float32,
        )
        produced[first : first + group] = made.astype(jnp.bfloat16).reshape(group, cap, width)
        for i in reversed(range(max(first, 1), first + group)):
            copy = remote(
                produced.at[i],
                returned.at[i],
                back_send.at[i],
                back_recv.at[i],
                {"exp": exp_at(n_exp - offsets[i])},
            )
            copy.start()
            pending.append(copy)
    returned[0] = produced[0]
    for i in range(1, n_exp):
        remote(produced.at[i], returned.at[i], back_send.at[i], back_recv.at[i], {"exp": exp_at(offsets[i])}).wait_recv()
    moe = jnp.dot(combine, returned[...].reshape(rows, width), preferred_element_type=jnp.float32)
    out[0] = (wide + moe).astype(jnp.bfloat16)
    for copy in pending:
        copy.wait_send()


def on_device(
    residual, query_rows, key_rows, value_rows, out_proj, router, expert_ids, expert_gate_up, expert_down
):
    n_ctx = lax.axis_size("ctx")
    n_exp = lax.axis_size("exp")
    chips = n_ctx // 2
    _, tok, width = residual.shape
    cap = min(tok, -(-(3 * tok // n_exp) // 16) * 16)
    bf16 = jnp.bfloat16
    depth, twice_ff = expert_gate_up.shape[1:]
    ff_part = expert_down.shape[1]
    half = out_proj.shape[0] // 2
    vmem = pl.BlockSpec(memory_space=pltpu.VMEM)
    anywhere = pl.BlockSpec(memory_space=pl.ANY)
    dma = pltpu.SemaphoreType.DMA
    ctx_sems = [dma((2 * chips,)), dma((n_ctx,))]
    rows = n_exp * cap
    groups = 4
    return pl.pallas_call(
        functools.partial(fused, n_ctx, n_exp, cap),
        out_shape=jax.ShapeDtypeStruct(residual.shape, bf16),
        in_specs=[anywhere] * 9,
        out_specs=vmem,
        scratch_shapes=[
            pltpu.VMEM((tok, width), bf16),
            pltpu.VMEM((tok, width), bf16),
            pltpu.VMEM((n_exp, width), bf16),
            pltpu.VMEM((2, tok), jnp.int32),
            pltpu.VMEM((n_ctx, 2 * groups, tok, width // groups), bf16),
            pltpu.VMEM((n_exp, 2, half, width), bf16),
            pltpu.VMEM((n_ctx, depth, twice_ff), bf16),
            pltpu.VMEM((n_ctx, ff_part, width), bf16),
            pltpu.VMEM((n_exp, cap, width), bf16),
            pltpu.VMEM((n_exp, cap, width), bf16),
            pltpu.VMEM((n_exp, cap, width), bf16),
            pltpu.VMEM((n_exp, cap, width), bf16),
            pltpu.VMEM((tok, width), bf16),
            pltpu.VMEM((rows, twice_ff // 2), bf16),
            dma((8,)),
            dma((2 * groups,)),
            dma((2 * groups, 2 * chips)),
            dma((2 * groups, n_ctx)),
        ]
        + ctx_sems * 2
        + [dma((n_exp,)), dma((n_exp, 2)), dma((n_exp,))]
        + [dma((n_exp,))] * 4,
        compiler_params=pltpu.CompilerParams(
            collective_id=0, has_side_effects=True, vmem_limit_bytes=60 * 1024 * 1024
        ),
    )(
        residual,
        query_rows,
        router.T,
        jnp.swapaxes(expert_ids, 1, 2),
        key_rows,
        value_rows,
        out_proj,
        expert_gate_up,
        expert_down,
    )


def solution(mesh):
    return jax.shard_map(
        on_device,
        mesh=mesh,
        in_specs=(
            P("exp", "ctx", None),
            P("exp", "ctx", None),
            P("exp", "ctx", None),
            P("exp", "ctx", None),
            P("exp", None),
            P(),
            P("exp", "ctx", None),
            P("exp", "ctx", None),
            P("exp", "ctx", None),
        ),
        out_specs=P("exp", "ctx", None),
        check_vma=False,
    )
```

```python
import functools

import jax
import jax.numpy as jnp
from jax import lax
from jax.experimental import pallas as pl
from jax.experimental.pallas import tpu as pltpu
from jax.sharding import PartitionSpec as P

HEADS = 8
HEAD_DIM = 128
NEG_FILL = -1e30
MESH = pl.DeviceIdType.MESH


def fused(
    n_ctx,
    n_exp,
    cap,
    residual_in,
    query_in,
    router_in,
    ids_in,
    key,
    value,
    out_proj,
    gate_up,
    down,
    out,
    residual,
    query,
    router,
    ids_ref,
    kvbuf,
    proj,
    gbuf,
    dbuf,
    outgoing,
    arrived,
    produced,
    returned,
    context,
    activation,
    local_sem,
    kv_local,
    kv_send,
    kv_recv,
    g_send,
    g_recv,
    d_send,
    d_recv,
    proj_send,
    proj_recv,
    proj_fwd,
    out_send,
    out_recv,
    back_send,
    back_recv,
):
    chips = n_ctx // 2
    c = lax.axis_index("ctx")
    e = lax.axis_index("exp")
    chip = c // 2
    core = lax.rem(c, 2)
    sibling = chip * 2 + 1 - core
    tok, width = query.shape
    groups = kvbuf.shape[1] // 2
    group_cols = kvbuf.shape[3]
    half = out_proj.shape[0] // 2
    part_depth = gbuf.shape[2]

    def chip_at(r):
        return lax.rem(chip + r, chips) * 2 + core

    def exp_at(r):
        return lax.rem(e + r, n_exp)

    barrier = pltpu.get_barrier_semaphore()
    for r in range(1, n_exp):
        pl.semaphore_signal(barrier, inc=1, device_id={"exp": exp_at(r)}, device_id_type=MESH)
    for r in range(1, chips):
        pl.semaphore_signal(barrier, inc=1, device_id={"ctx": chip_at(r)}, device_id_type=MESH)
    pl.semaphore_signal(barrier, inc=1, device_id={"ctx": sibling}, device_id_type=MESH)

    locals_ = [
        pltpu.make_async_copy(query_in.at[0], query, local_sem.at[0]),
        pltpu.make_async_copy(residual_in.at[0], residual, local_sem.at[1]),
        pltpu.make_async_copy(out_proj.at[pl.ds(0, half)], proj.at[e, 0], local_sem.at[2]),
        pltpu.make_async_copy(out_proj.at[pl.ds(half, half)], proj.at[e, 1], local_sem.at[3]),
        pltpu.make_async_copy(gate_up.at[0, pl.ds(0, part_depth)], gbuf.at[c, 0], local_sem.at[4]),
        pltpu.make_async_copy(gate_up.at[0, pl.ds(part_depth, part_depth)], gbuf.at[c, 1], local_sem.at[8]),
        pltpu.make_async_copy(down.at[0], dbuf.at[c], local_sem.at[5]),
        pltpu.make_async_copy(router_in, router, local_sem.at[6]),
        pltpu.make_async_copy(ids_in.at[0], ids_ref, local_sem.at[7]),
    ]
    kv_parts = []
    for g in range(groups):
        for ref in (key, value):
            kv_parts.append(ref.at[0, :, pl.ds(g * group_cols, group_cols)])
    for i, part in enumerate(kv_parts):
        locals_.append(pltpu.make_async_copy(part, kvbuf.at[c, i], kv_local.at[i]))
    for copy in locals_:
        copy.start()
    pl.semaphore_wait(barrier, n_exp - 1 + chips - 1 + 1)

    pending = []

    def remote(src, dst, send, recv, where):
        return pltpu.make_async_remote_copy(
            src_ref=src, dst_ref=dst, send_sem=send, recv_sem=recv, device_id=where, device_id_type=MESH
        )

    def spread(src, buf, send, recv):
        copies = []
        for r in range(1, chips):
            copies.append(remote(src, buf.at[c], send.at[r - 1], recv.at[c], {"ctx": chip_at(r)}))
        copies.append(remote(src, buf.at[c], send.at[chips - 1], recv.at[c], {"ctx": sibling}))
        for copy in copies:
            copy.start()
        return copies

    def landed(buf, send, recv, s):
        remote(buf.at[s], buf.at[s], send.at[0], recv.at[s], {"ctx": sibling}).wait_recv()

    def forward(buf, send, recv):
        for r in range(1, chips):
            s = chip_at(chips - r)
            landed(buf, send, recv, s)
            copy = remote(buf.at[s], buf.at[s], send.at[chips - 1 + r], recv.at[s], {"ctx": sibling})
            copy.start()
            pending.append(copy)

    def from_sibling(buf, send, recv):
        for r in range(chips):
            landed(buf, send, recv, lax.rem(chip + r, chips) * 2 + 1 - core)

    kv_copies = {}
    kv_views = [(kvbuf.at[:, i], kv_send.at[i], kv_recv.at[i]) for i in range(2 * groups)]

    def send_group(g):
        kv_copies[g] = spread(kv_parts[2 * g], *kv_views[2 * g]) + spread(kv_parts[2 * g + 1], *kv_views[2 * g + 1])

    send_group(0)
    send_group(1)
    offsets = [0]
    for r in range(1, n_exp // 2 + 1):
        offsets.append(r)
        if n_exp - r != r:
            offsets.append(n_exp - r)
    own_half = out_proj.at[pl.ds(pl.multiple_of(core * half, half), half)]
    for r in reversed(offsets[1:]):
        copy = remote(own_half, proj.at[e, core], proj_send.at[r], proj_recv.at[e, core], {"exp": exp_at(r)})
        copy.start()
        pending.append(copy)

    gate_parts = [gate_up.at[0, pl.ds(i * part_depth, part_depth)] for i in range(2)]
    gate_views = [(gbuf.at[:, i], g_send.at[i], g_recv.at[i]) for i in range(2)]

    def proj_at(s, side):
        return remote(proj.at[s, side], proj.at[s, side], proj_fwd.at[s], proj_recv.at[s, side], {"ctx": sibling})

    for copy in locals_:
        copy.wait()
    keys = n_ctx * tok
    q_pos = c * tok + lax.broadcasted_iota(jnp.int32, (tok, keys), 0)
    k_pos = lax.broadcasted_iota(jnp.int32, (tok, keys), 1)
    allowed = k_pos <= q_pos
    for g in range(groups):
        forward(*kv_views[2 * g])
        forward(*kv_views[2 * g + 1])
        for copy in kv_copies[g]:
            copy.wait_send()
        if g + 2 < groups:
            send_group(g + 2)
        if g == groups - 2:
            first_half = spread(gate_parts[0], *gate_views[0])
        if g == groups - 1:
            pending.extend(spread(gate_parts[1], *gate_views[1]))
            for r in offsets[1:]:
                s = exp_at(r)
                proj_at(s, core).wait_recv()
                copy = proj_at(s, core)
                copy.start()
                pending.append(copy)
        from_sibling(*kv_views[2 * g])
        from_sibling(*kv_views[2 * g + 1])
        for h in range(group_cols // HEAD_DIM):
            inner = slice(h * HEAD_DIM, (h + 1) * HEAD_DIM)
            cols = slice(g * group_cols + h * HEAD_DIM, g * group_cols + (h + 1) * HEAD_DIM)
            k_head = kvbuf[:, 2 * g, :, inner].reshape(keys, HEAD_DIM)
            v_head = kvbuf[:, 2 * g + 1, :, inner].reshape(keys, HEAD_DIM)
            scores = lax.dot_general(
                query[:, cols], k_head, (((1,), (1,)), ((), ())), preferred_element_type=jnp.float32
            )
            scores = jnp.where(allowed, scores * (HEAD_DIM**-0.5), NEG_FILL)
            weights = jnp.exp(scores - jnp.max(scores, axis=1, keepdims=True))
            total = jnp.sum(weights, axis=1, keepdims=True)
            part = jnp.dot(weights.astype(jnp.bfloat16), v_head, preferred_element_type=jnp.float32)
            context[:, cols] = (part / total).astype(jnp.bfloat16)

    for r in offsets[1:]:
        proj_at(exp_at(r), 1 - core).wait_recv()
    attn_out = jnp.dot(
        context[...], proj[...].reshape(n_exp * 2 * half, width), preferred_element_type=jnp.float32
    )
    hidden = (residual[...].astype(jnp.float32) + attn_out).astype(jnp.bfloat16)
    wide = hidden.astype(jnp.float32)
    mean_square = jnp.mean(wide * wide, axis=1, keepdims=True)
    normed = (wide * lax.rsqrt(mean_square + 1e-06)).astype(jnp.bfloat16)

    eye = jnp.where(
        lax.broadcasted_iota(jnp.int32, (tok, tok), 1) == lax.broadcasted_iota(jnp.int32, (tok, tok), 0), 1.0, 0.0
    ).astype(jnp.bfloat16)
    ids = lax.dot_general(
        eye,
        ids_ref[...].astype(jnp.float32).astype(jnp.bfloat16),
        (((1,), (1,)), ((), ())),
        preferred_element_type=jnp.float32,
    ).astype(jnp.int32)
    slots = []
    for k in range(2):
        away = ids[:, k : k + 1] - e
        away = jnp.where(away < 0, away + n_exp, away)
        slot = jnp.where(2 * away <= n_exp, 2 * away - 1, 2 * (n_exp - away))
        slots.append(jnp.where(away == 0, 0, slot))
    lane = lax.broadcasted_iota(jnp.int32, (tok, 128), 1)
    picks = [lane == slots[k] for k in range(2)]
    member = jnp.where(picks[0] | picks[1], 1.0, 0.0)
    below = jnp.where(
        lax.broadcasted_iota(jnp.int32, (tok, tok), 1) < lax.broadcasted_iota(jnp.int32, (tok, tok), 0), 1.0, 0.0
    ).astype(jnp.bfloat16)
    rank = jnp.dot(below, member.astype(jnp.bfloat16), preferred_element_type=jnp.float32)
    place = (member * (rank + 1.0)).astype(jnp.bfloat16)
    grid = (n_exp, cap, 128)
    rows = n_exp * cap
    spread_out = jnp.where(
        lax.broadcasted_iota(jnp.int32, grid, 0) == lax.broadcasted_iota(jnp.int32, grid, 2), 1.0, 0.0
    ).reshape(rows, 128)
    wanted = (lax.broadcasted_iota(jnp.int32, (n_exp, cap, tok), 1) + 1).astype(jnp.float32).reshape(rows, tok)
    held = lax.dot_general(
        spread_out.astype(jnp.bfloat16), place, (((1,), (1,)), ((), ())), preferred_element_type=jnp.float32
    )
    dispatch = jnp.where(held == wanted, 1.0, 0.0).astype(jnp.bfloat16)
    sent = jnp.dot(dispatch, normed, preferred_element_type=jnp.float32).astype(jnp.bfloat16)
    outgoing[...] = sent.reshape(n_exp, cap, width)
    for i in reversed(range(1, n_exp)):
        copy = remote(
            outgoing.at[i], arrived.at[i], out_send.at[i], out_recv.at[i], {"exp": exp_at(offsets[i])}
        )
        copy.start()
        pending.append(copy)
    arrived[0] = outgoing[0]

    affinity = jax.nn.sigmoid(
        lax.dot_general(normed, router[...], (((1,), (1,)), ((), ())), preferred_element_type=jnp.float32)
    )
    expert_lane = lax.broadcasted_iota(jnp.int32, affinity.shape, 1)
    picked = [
        jnp.sum(jnp.where(expert_lane == ids[:, k : k + 1], affinity, 0.0), axis=1, keepdims=True) for k in range(2)
    ]
    both = picked[0] + picked[1]
    column = lax.broadcasted_iota(jnp.int32, (tok, rows), 1).astype(jnp.float32)
    combine = jnp.zeros((tok, rows), jnp.float32)
    for k in range(2):
        own_rank = jnp.sum(jnp.where(picks[k], rank, 0.0), axis=1, keepdims=True)
        target = slots[k].astype(jnp.float32) * cap + own_rank
        combine = combine + jnp.where(column == target, picked[k] / both, 0.0)
    combine = combine.astype(jnp.bfloat16)

    for copy in first_half:
        copy.wait_send()
    forward(*gate_views[0])
    pending.extend(spread(down.at[0], dbuf, d_send, d_recv))
    forward(*gate_views[1])
    from_sibling(*gate_views[0])
    from_sibling(*gate_views[1])
    ff = activation.shape[1]
    group = n_exp // 2
    chunk = 256
    for first in range(0, n_exp, group):
        for i in range(max(first, 1), first + group):
            remote(
                outgoing.at[i], arrived.at[i], out_send.at[i], out_recv.at[i], {"exp": exp_at(offsets[i])}
            ).wait_recv()
        feats = arrived[first : first + group].reshape(group * cap, width)
        for f in range(0, ff, chunk):
            gate = jnp.dot(
                feats, gbuf[:, :, :, f : f + chunk].reshape(width, chunk), preferred_element_type=jnp.float32
            )
            up = jnp.dot(
                feats, gbuf[:, :, :, ff + f : ff + f + chunk].reshape(width, chunk), preferred_element_type=jnp.float32
            )
            activation[first * cap : (first + group) * cap, f : f + chunk] = (
                gate / (1.0 + jnp.exp(-gate)) * up
            ).astype(jnp.bfloat16)
    forward(dbuf, d_send, d_recv)
    from_sibling(dbuf, d_send, d_recv)
    for first in (group, 0):
        made = jnp.dot(
            activation[first * cap : (first + group) * cap],
            dbuf[...].reshape(ff, width),
            preferred_element_type=jnp.float32,
        )
        produced[first : first + group] = made.astype(jnp.bfloat16).reshape(group, cap, width)
        for i in reversed(range(max(first, 1), first + group)):
            copy = remote(
                produced.at[i],
                returned.at[i],
                back_send.at[i],
                back_recv.at[i],
                {"exp": exp_at(n_exp - offsets[i])},
            )
            copy.start()
            pending.append(copy)
    returned[0] = produced[0]
    for i in range(1, n_exp):
        remote(produced.at[i], returned.at[i], back_send.at[i], back_recv.at[i], {"exp": exp_at(offsets[i])}).wait_recv()
    moe = jnp.dot(combine, returned[...].reshape(rows, width), preferred_element_type=jnp.float32)
    out[0] = (wide + moe).astype(jnp.bfloat16)
    for copy in pending:
        copy.wait_send()


def on_device(
    residual, query_rows, key_rows, value_rows, out_proj, router, expert_ids, expert_gate_up, expert_down
):
    n_ctx = lax.axis_size("ctx")
    n_exp = lax.axis_size("exp")
    chips = n_ctx // 2
    _, tok, width = residual.shape
    cap = min(tok, -(-(3 * tok // n_exp) // 16) * 16)
    bf16 = jnp.bfloat16
    depth, twice_ff = expert_gate_up.shape[1:]
    ff_part = expert_down.shape[1]
    half = out_proj.shape[0] // 2
    vmem = pl.BlockSpec(memory_space=pltpu.VMEM)
    anywhere = pl.BlockSpec(memory_space=pl.ANY)
    dma = pltpu.SemaphoreType.DMA
    ctx_sems = [dma((2 * chips,)), dma((n_ctx,))]
    rows = n_exp * cap
    groups = 4
    return pl.pallas_call(
        functools.partial(fused, n_ctx, n_exp, cap),
        out_shape=jax.ShapeDtypeStruct(residual.shape, bf16),
        in_specs=[anywhere] * 9,
        out_specs=vmem,
        scratch_shapes=[
            pltpu.VMEM((tok, width), bf16),
            pltpu.VMEM((tok, width), bf16),
            pltpu.VMEM((n_exp, width), bf16),
            pltpu.VMEM((2, tok), jnp.int32),
            pltpu.VMEM((n_ctx, 2 * groups, tok, width // groups), bf16),
            pltpu.VMEM((n_exp, 2, half, width), bf16),
            pltpu.VMEM((n_ctx, 2, depth // 2, twice_ff), bf16),
            pltpu.VMEM((n_ctx, ff_part, width), bf16),
            pltpu.VMEM((n_exp, cap, width), bf16),
            pltpu.VMEM((n_exp, cap, width), bf16),
            pltpu.VMEM((n_exp, cap, width), bf16),
            pltpu.VMEM((n_exp, cap, width), bf16),
            pltpu.VMEM((tok, width), bf16),
            pltpu.VMEM((rows, twice_ff // 2), bf16),
            dma((9,)),
            dma((2 * groups,)),
            dma((2 * groups, 2 * chips)),
            dma((2 * groups, n_ctx)),
        ]
        + [dma((2, 2 * chips)), dma((2, n_ctx))]
        + ctx_sems
        + [dma((n_exp,)), dma((n_exp, 2)), dma((n_exp,))]
        + [dma((n_exp,))] * 4,
        compiler_params=pltpu.CompilerParams(
            collective_id=0, has_side_effects=True, vmem_limit_bytes=60 * 1024 * 1024
        ),
    )(
        residual,
        query_rows,
        router.T,
        jnp.swapaxes(expert_ids, 1, 2),
        key_rows,
        value_rows,
        out_proj,
        expert_gate_up,
        expert_down,
    )


def solution(mesh):
    return jax.shard_map(
        on_device,
        mesh=mesh,
        in_specs=(
            P("exp", "ctx", None),
            P("exp", "ctx", None),
            P("exp", "ctx", None),
            P("exp", "ctx", None),
            P("exp", None),
            P(),
            P("exp", "ctx", None),
            P("exp", "ctx", None),
            P("exp", "ctx", None),
        ),
        out_specs=P("exp", "ctx", None),
        check_vma=False,
    )
```

```python
import functools

import jax
import jax.numpy as jnp
from jax import lax
from jax.experimental import pallas as pl
from jax.experimental.pallas import tpu as pltpu
from jax.sharding import PartitionSpec as P

HEADS = 8
HEAD_DIM = 128
NEG_FILL = -1e30
MESH = pl.DeviceIdType.MESH


def fused(
    n_ctx,
    n_exp,
    cap,
    residual_in,
    query_in,
    router_in,
    ids_in,
    key,
    value,
    out_proj,
    gate_up,
    down,
    returned,
    hidden_out,
    combine_out,
    residual,
    query,
    router,
    ids_ref,
    kvbuf,
    proj,
    gbuf,
    dbuf,
    outgoing,
    arrived,
    produced,
    dispatch,
    chosen,
    hidden_part,
    combine_part,
    context,
    activation,
    local_sem,
    kv_local,
    kv_send,
    kv_recv,
    g_send,
    g_recv,
    d_send,
    d_recv,
    proj_send,
    proj_recv,
    proj_fwd,
    out_send,
    out_recv,
    back_send,
    back_recv,
):
    chips = n_ctx // 2
    c = lax.axis_index("ctx")
    e = lax.axis_index("exp")
    chip = c // 2
    core = lax.rem(c, 2)
    sibling = chip * 2 + 1 - core
    tok, width = query.shape
    groups = kvbuf.shape[1] // 2
    group_cols = kvbuf.shape[3]
    half = out_proj.shape[0] // 2
    part_depth = gbuf.shape[2]

    def chip_at(r):
        return lax.rem(chip + r, chips) * 2 + core

    def exp_at(r):
        return lax.rem(e + r, n_exp)

    barrier = pltpu.get_barrier_semaphore()
    for r in range(1, n_exp):
        pl.semaphore_signal(barrier, inc=1, device_id={"exp": exp_at(r)}, device_id_type=MESH)
    for r in range(1, chips):
        pl.semaphore_signal(barrier, inc=1, device_id={"ctx": chip_at(r)}, device_id_type=MESH)
    pl.semaphore_signal(barrier, inc=1, device_id={"ctx": sibling}, device_id_type=MESH)

    locals_ = [
        pltpu.make_async_copy(query_in.at[0], query, local_sem.at[0]),
        pltpu.make_async_copy(residual_in.at[0], residual, local_sem.at[1]),
        pltpu.make_async_copy(out_proj.at[pl.ds(0, half)], proj.at[e, 0], local_sem.at[2]),
        pltpu.make_async_copy(out_proj.at[pl.ds(half, half)], proj.at[e, 1], local_sem.at[3]),
        pltpu.make_async_copy(gate_up.at[0, pl.ds(0, part_depth)], gbuf.at[c, 0], local_sem.at[4]),
        pltpu.make_async_copy(gate_up.at[0, pl.ds(part_depth, part_depth)], gbuf.at[c, 1], local_sem.at[8]),
        pltpu.make_async_copy(down.at[0], dbuf.at[c], local_sem.at[5]),
        pltpu.make_async_copy(router_in, router, local_sem.at[6]),
        pltpu.make_async_copy(ids_in.at[0], ids_ref, local_sem.at[7]),
    ]
    kv_parts = []
    for g in range(groups):
        for ref in (key, value):
            kv_parts.append(ref.at[0, :, pl.ds(g * group_cols, group_cols)])
    for i, part in enumerate(kv_parts):
        locals_.append(pltpu.make_async_copy(part, kvbuf.at[c, i], kv_local.at[i]))
    for copy in locals_:
        copy.start()
    pl.semaphore_wait(barrier, n_exp - 1 + chips - 1 + 1)

    pending = []

    def remote(src, dst, send, recv, where):
        return pltpu.make_async_remote_copy(
            src_ref=src, dst_ref=dst, send_sem=send, recv_sem=recv, device_id=where, device_id_type=MESH
        )

    def spread(src, buf, send, recv):
        copies = []
        for r in range(1, chips):
            copies.append(remote(src, buf.at[c], send.at[r - 1], recv.at[c], {"ctx": chip_at(r)}))
        copies.append(remote(src, buf.at[c], send.at[chips - 1], recv.at[c], {"ctx": sibling}))
        for copy in copies:
            copy.start()
        return copies

    def landed(buf, send, recv, s):
        remote(buf.at[s], buf.at[s], send.at[0], recv.at[s], {"ctx": sibling}).wait_recv()

    def forward(buf, send, recv):
        for r in range(1, chips):
            s = chip_at(chips - r)
            landed(buf, send, recv, s)
            copy = remote(buf.at[s], buf.at[s], send.at[chips - 1 + r], recv.at[s], {"ctx": sibling})
            copy.start()
            pending.append(copy)

    def from_sibling(buf, send, recv):
        for r in range(chips):
            landed(buf, send, recv, lax.rem(chip + r, chips) * 2 + 1 - core)

    kv_copies = {}
    kv_views = [(kvbuf.at[:, i], kv_send.at[i], kv_recv.at[i]) for i in range(2 * groups)]

    def send_group(g):
        kv_copies[g] = spread(kv_parts[2 * g], *kv_views[2 * g]) + spread(kv_parts[2 * g + 1], *kv_views[2 * g + 1])

    send_group(0)
    send_group(1)
    offsets = [0]
    for r in range(1, n_exp // 2 + 1):
        offsets.append(r)
        if n_exp - r != r:
            offsets.append(n_exp - r)
    own_half = out_proj.at[pl.ds(pl.multiple_of(core * half, half), half)]
    for r in reversed(offsets[1:]):
        copy = remote(own_half, proj.at[e, core], proj_send.at[r], proj_recv.at[e, core], {"exp": exp_at(r)})
        copy.start()
        pending.append(copy)

    gate_parts = [gate_up.at[0, pl.ds(i * part_depth, part_depth)] for i in range(2)]
    gate_views = [(gbuf.at[:, i], g_send.at[i], g_recv.at[i]) for i in range(2)]

    def proj_at(s, side):
        return remote(proj.at[s, side], proj.at[s, side], proj_fwd.at[s], proj_recv.at[s, side], {"ctx": sibling})

    for copy in locals_:
        copy.wait()

    eye = jnp.where(
        lax.broadcasted_iota(jnp.int32, (tok, tok), 1) == lax.broadcasted_iota(jnp.int32, (tok, tok), 0), 1.0, 0.0
    ).astype(jnp.bfloat16)
    ids = lax.dot_general(
        eye,
        ids_ref[...].astype(jnp.float32).astype(jnp.bfloat16),
        (((1,), (1,)), ((), ())),
        preferred_element_type=jnp.float32,
    ).astype(jnp.int32)
    slots = []
    for k in range(2):
        away = ids[:, k : k + 1] - e
        away = jnp.where(away < 0, away + n_exp, away)
        slot = jnp.where(2 * away <= n_exp, 2 * away - 1, 2 * (n_exp - away))
        slots.append(jnp.where(away == 0, 0, slot))
    lane = lax.broadcasted_iota(jnp.int32, (tok, 128), 1)
    picks = [lane == slots[k] for k in range(2)]
    member = jnp.where(picks[0] | picks[1], 1.0, 0.0)
    below = jnp.where(
        lax.broadcasted_iota(jnp.int32, (tok, tok), 1) < lax.broadcasted_iota(jnp.int32, (tok, tok), 0), 1.0, 0.0
    ).astype(jnp.bfloat16)
    rank = jnp.dot(below, member.astype(jnp.bfloat16), preferred_element_type=jnp.float32)
    place = (member * (rank + 1.0)).astype(jnp.bfloat16)
    grid = (n_exp, cap, 128)
    rows = n_exp * cap
    spread_out = jnp.where(
        lax.broadcasted_iota(jnp.int32, grid, 0) == lax.broadcasted_iota(jnp.int32, grid, 2), 1.0, 0.0
    ).reshape(rows, 128)
    wanted = (lax.broadcasted_iota(jnp.int32, (n_exp, cap, tok), 1) + 1).astype(jnp.float32).reshape(rows, tok)
    held = lax.dot_general(
        spread_out.astype(jnp.bfloat16), place, (((1,), (1,)), ((), ())), preferred_element_type=jnp.float32
    )
    dispatch[...] = jnp.where(held == wanted, 1.0, 0.0).astype(jnp.bfloat16)
    column = lax.broadcasted_iota(jnp.int32, (tok, rows), 1).astype(jnp.float32)
    for k in range(2):
        own_rank = jnp.sum(jnp.where(picks[k], rank, 0.0), axis=1, keepdims=True)
        target = slots[k].astype(jnp.float32) * cap + own_rank
        chosen[k] = jnp.where(column == target, 1.0, 0.0)

    keys = n_ctx * tok
    q_pos = c * tok + lax.broadcasted_iota(jnp.int32, (tok, keys), 0)
    k_pos = lax.broadcasted_iota(jnp.int32, (tok, keys), 1)
    allowed = k_pos <= q_pos
    for g in range(groups):
        forward(*kv_views[2 * g])
        forward(*kv_views[2 * g + 1])
        for copy in kv_copies[g]:
            copy.wait_send()
        if g + 2 < groups:
            send_group(g + 2)
        if g == groups - 2:
            first_half = spread(gate_parts[0], *gate_views[0])
        if g == groups - 1:
            pending.extend(spread(gate_parts[1], *gate_views[1]))
            for r in offsets[1:]:
                s = exp_at(r)
                proj_at(s, core).wait_recv()
                copy = proj_at(s, core)
                copy.start()
                pending.append(copy)
        from_sibling(*kv_views[2 * g])
        from_sibling(*kv_views[2 * g + 1])
        for h in range(group_cols // HEAD_DIM):
            inner = slice(h * HEAD_DIM, (h + 1) * HEAD_DIM)
            cols = slice(g * group_cols + h * HEAD_DIM, g * group_cols + (h + 1) * HEAD_DIM)
            k_head = kvbuf[:, 2 * g, :, inner].reshape(keys, HEAD_DIM)
            v_head = kvbuf[:, 2 * g + 1, :, inner].reshape(keys, HEAD_DIM)
            scores = lax.dot_general(
                query[:, cols], k_head, (((1,), (1,)), ((), ())), preferred_element_type=jnp.float32
            )
            scores = jnp.where(allowed, scores * (HEAD_DIM**-0.5), NEG_FILL)
            weights = jnp.exp(scores - jnp.max(scores, axis=1, keepdims=True))
            total = jnp.sum(weights, axis=1, keepdims=True)
            part = jnp.dot(weights.astype(jnp.bfloat16), v_head, preferred_element_type=jnp.float32)
            context[:, cols] = (part / total).astype(jnp.bfloat16)

    for r in offsets[1:]:
        proj_at(exp_at(r), 1 - core).wait_recv()
    attn_out = jnp.dot(
        context[...], proj[...].reshape(n_exp * 2 * half, width), preferred_element_type=jnp.float32
    )
    hidden = (residual[...].astype(jnp.float32) + attn_out).astype(jnp.bfloat16)
    hidden_part[...] = hidden
    wide = hidden.astype(jnp.float32)
    mean_square = jnp.mean(wide * wide, axis=1, keepdims=True)
    normed = (wide * lax.rsqrt(mean_square + 1e-06)).astype(jnp.bfloat16)

    group = n_exp // 2
    for first in (group, 0):
        sent = jnp.dot(
            dispatch[first * cap : (first + group) * cap], normed, preferred_element_type=jnp.float32
        ).astype(jnp.bfloat16)
        outgoing[first : first + group] = sent.reshape(group, cap, width)
        for i in reversed(range(max(first, 1), first + group)):
            copy = remote(
                outgoing.at[i], arrived.at[i], out_send.at[i], out_recv.at[i], {"exp": exp_at(offsets[i])}
            )
            copy.start()
            pending.append(copy)
    arrived[0] = outgoing[0]

    affinity = jax.nn.sigmoid(
        lax.dot_general(normed, router[...], (((1,), (1,)), ((), ())), preferred_element_type=jnp.float32)
    )
    expert_lane = lax.broadcasted_iota(jnp.int32, affinity.shape, 1)
    picked = [
        jnp.sum(jnp.where(expert_lane == ids[:, k : k + 1], affinity, 0.0), axis=1, keepdims=True) for k in range(2)
    ]
    both = picked[0] + picked[1]
    combine = jnp.zeros((tok, rows), jnp.float32)
    for k in range(2):
        combine = combine + chosen[k] * (picked[k] / both)
    combine_part[...] = combine.astype(jnp.bfloat16)
    results = [
        pltpu.make_async_copy(hidden_part, hidden_out, local_sem.at[9]),
        pltpu.make_async_copy(combine_part, combine_out, local_sem.at[10]),
    ]
    for copy in results:
        copy.start()

    for copy in first_half:
        copy.wait_send()
    forward(*gate_views[0])
    pending.extend(spread(down.at[0], dbuf, d_send, d_recv))
    forward(*gate_views[1])
    from_sibling(*gate_views[0])
    from_sibling(*gate_views[1])
    ff = activation.shape[1]
    chunk = 256
    for first in (0, group):
        if first == group:
            forward(dbuf, d_send, d_recv)
        for i in range(max(first, 1), first + group):
            remote(
                outgoing.at[i], arrived.at[i], out_send.at[i], out_recv.at[i], {"exp": exp_at(offsets[i])}
            ).wait_recv()
        feats = arrived[first : first + group].reshape(group * cap, width)
        for f in range(0, ff, chunk):
            gate = jnp.dot(
                feats, gbuf[:, :, :, f : f + chunk].reshape(width, chunk), preferred_element_type=jnp.float32
            )
            up = jnp.dot(
                feats, gbuf[:, :, :, ff + f : ff + f + chunk].reshape(width, chunk), preferred_element_type=jnp.float32
            )
            activation[first * cap : (first + group) * cap, f : f + chunk] = (
                gate / (1.0 + jnp.exp(-gate)) * up
            ).astype(jnp.bfloat16)
    from_sibling(dbuf, d_send, d_recv)
    for first in (group, 0):
        made = jnp.dot(
            activation[first * cap : (first + group) * cap],
            dbuf[...].reshape(ff, width),
            preferred_element_type=jnp.float32,
        )
        produced[first : first + group] = made.astype(jnp.bfloat16).reshape(group, cap, width)
        for i in reversed(range(max(first, 1), first + group)):
            copy = remote(
                produced.at[i],
                returned.at[i],
                back_send.at[i],
                back_recv.at[i],
                {"exp": exp_at(n_exp - offsets[i])},
            )
            copy.start()
            pending.append(copy)
    own = pltpu.make_async_copy(produced.at[0], returned.at[0], local_sem.at[11])
    own.start()
    results.append(own)
    for i in range(1, n_exp):
        remote(produced.at[i], returned.at[i], back_send.at[i], back_recv.at[i], {"exp": exp_at(offsets[i])}).wait_recv()
    for copy in results:
        copy.wait()
    for copy in pending:
        copy.wait_send()


def on_device(
    residual, query_rows, key_rows, value_rows, out_proj, router, expert_ids, expert_gate_up, expert_down
):
    n_ctx = lax.axis_size("ctx")
    n_exp = lax.axis_size("exp")
    chips = n_ctx // 2
    _, tok, width = residual.shape
    cap = min(tok, -(-(3 * tok // n_exp) // 16) * 16)
    bf16 = jnp.bfloat16
    depth, twice_ff = expert_gate_up.shape[1:]
    ff_part = expert_down.shape[1]
    half = out_proj.shape[0] // 2
    anywhere = pl.BlockSpec(memory_space=pl.ANY)
    dma = pltpu.SemaphoreType.DMA
    ctx_sems = [dma((2 * chips,)), dma((n_ctx,))]
    rows = n_exp * cap
    groups = 4
    returned, hidden, combine = pl.pallas_call(
        functools.partial(fused, n_ctx, n_exp, cap),
        out_shape=[
            jax.ShapeDtypeStruct((n_exp, cap, width), bf16),
            jax.ShapeDtypeStruct((tok, width), bf16),
            jax.ShapeDtypeStruct((tok, rows), bf16),
        ],
        in_specs=[anywhere] * 9,
        out_specs=[anywhere] * 3,
        scratch_shapes=[
            pltpu.VMEM((tok, width), bf16),
            pltpu.VMEM((tok, width), bf16),
            pltpu.VMEM((n_exp, width), bf16),
            pltpu.VMEM((2, tok), jnp.int32),
            pltpu.VMEM((n_ctx, 2 * groups, tok, width // groups), bf16),
            pltpu.VMEM((n_exp, 2, half, width), bf16),
            pltpu.VMEM((n_ctx, 2, depth // 2, twice_ff), bf16),
            pltpu.VMEM((n_ctx, ff_part, width), bf16),
            pltpu.VMEM((n_exp, cap, width), bf16),
            pltpu.VMEM((n_exp, cap, width), bf16),
            pltpu.VMEM((n_exp, cap, width), bf16),
            pltpu.VMEM((rows, tok), bf16),
            pltpu.VMEM((2, tok, rows), jnp.float32),
            pltpu.VMEM((tok, width), bf16),
            pltpu.VMEM((tok, rows), bf16),
            pltpu.VMEM((tok, width), bf16),
            pltpu.VMEM((rows, twice_ff // 2), bf16),
            dma((12,)),
            dma((2 * groups,)),
            dma((2 * groups, 2 * chips)),
            dma((2 * groups, n_ctx)),
        ]
        + [dma((2, 2 * chips)), dma((2, n_ctx))]
        + ctx_sems
        + [dma((n_exp,)), dma((n_exp, 2)), dma((n_exp,))]
        + [dma((n_exp,))] * 4,
        compiler_params=pltpu.CompilerParams(
            collective_id=0, has_side_effects=True, vmem_limit_bytes=60 * 1024 * 1024
        ),
    )(
        residual,
        query_rows,
        router.T,
        jnp.swapaxes(expert_ids, 1, 2),
        key_rows,
        value_rows,
        out_proj,
        expert_gate_up,
        expert_down,
    )
    moe = jnp.dot(combine, returned.reshape(rows, width), preferred_element_type=jnp.float32)
    return (hidden.astype(jnp.float32) + moe).astype(bf16)[None]


def solution(mesh):
    return jax.shard_map(
        on_device,
        mesh=mesh,
        in_specs=(
            P("exp", "ctx", None),
            P("exp", "ctx", None),
            P("exp", "ctx", None),
            P("exp", "ctx", None),
            P("exp", None),
            P(),
            P("exp", "ctx", None),
            P("exp", "ctx", None),
            P("exp", "ctx", None),
        ),
        out_specs=P("exp", "ctx", None),
        check_vma=False,
    )
```

```python
import functools

import jax
import jax.numpy as jnp
from jax import lax
from jax.experimental import pallas as pl
from jax.experimental.pallas import tpu as pltpu
from jax.sharding import PartitionSpec as P

HEADS = 8
HEAD_DIM = 128
NEG_FILL = -1e30
MESH = pl.DeviceIdType.MESH


def fused(
    n_ctx,
    n_exp,
    cap,
    residual_in,
    query_in,
    router_in,
    ids_in,
    key,
    value,
    out_proj,
    gate_up,
    down,
    returned,
    hidden_out,
    combine_out,
    residual,
    query,
    router,
    ids_ref,
    kvbuf,
    proj,
    gbuf,
    dbuf,
    outgoing,
    arrived,
    produced,
    dispatch,
    chosen,
    hidden_part,
    combine_part,
    context,
    activation,
    local_sem,
    queries_in,
    part_out,
    part_in,
    stat_out,
    stat_in,
    own_part,
    kv_local,
    kv_send,
    kv_recv,
    q_send,
    q_recv,
    part_send,
    part_recv,
    stat_send,
    stat_recv,
    g_send,
    g_recv,
    d_send,
    d_recv,
    proj_send,
    proj_recv,
    proj_fwd,
    out_send,
    out_recv,
    back_send,
    back_recv,
):
    chips = n_ctx // 2
    c = lax.axis_index("ctx")
    e = lax.axis_index("exp")
    chip = c // 2
    core = lax.rem(c, 2)
    sibling = chip * 2 + 1 - core
    tok, width = query.shape
    half = out_proj.shape[0] // 2
    part_depth = gbuf.shape[2]

    def chip_at(r):
        return lax.rem(chip + r, chips) * 2 + core

    def exp_at(r):
        return lax.rem(e + r, n_exp)

    barrier = pltpu.get_barrier_semaphore()
    for r in range(1, n_exp):
        pl.semaphore_signal(barrier, inc=1, device_id={"exp": exp_at(r)}, device_id_type=MESH)
    for r in range(1, chips):
        pl.semaphore_signal(barrier, inc=1, device_id={"ctx": chip_at(r)}, device_id_type=MESH)
    pl.semaphore_signal(barrier, inc=1, device_id={"ctx": sibling}, device_id_type=MESH)

    locals_ = [
        pltpu.make_async_copy(query_in.at[0], query, local_sem.at[0]),
        pltpu.make_async_copy(residual_in.at[0], residual, local_sem.at[1]),
        pltpu.make_async_copy(out_proj.at[pl.ds(0, half)], proj.at[e, 0], local_sem.at[2]),
        pltpu.make_async_copy(out_proj.at[pl.ds(half, half)], proj.at[e, 1], local_sem.at[3]),
        pltpu.make_async_copy(gate_up.at[0, pl.ds(0, part_depth)], gbuf.at[c, 0], local_sem.at[4]),
        pltpu.make_async_copy(gate_up.at[0, pl.ds(part_depth, part_depth)], gbuf.at[c, 1], local_sem.at[8]),
        pltpu.make_async_copy(down.at[0], dbuf.at[c], local_sem.at[5]),
        pltpu.make_async_copy(router_in, router, local_sem.at[6]),
        pltpu.make_async_copy(ids_in.at[0], ids_ref, local_sem.at[7]),
    ]
    for i, ref in enumerate((key, value)):
        locals_.append(pltpu.make_async_copy(ref.at[0], kvbuf.at[i, core], kv_local.at[i]))
    for copy in locals_:
        copy.start()
    pl.semaphore_wait(barrier, n_exp - 1 + chips - 1 + 1)

    pending = []

    def remote(src, dst, send, recv, where):
        return pltpu.make_async_remote_copy(
            src_ref=src, dst_ref=dst, send_sem=send, recv_sem=recv, device_id=where, device_id_type=MESH
        )

    def spread(src, buf, send, recv):
        copies = []
        for r in range(1, chips):
            copies.append(remote(src, buf.at[c], send.at[r - 1], recv.at[c], {"ctx": chip_at(r)}))
        copies.append(remote(src, buf.at[c], send.at[chips - 1], recv.at[c], {"ctx": sibling}))
        for copy in copies:
            copy.start()
        return copies

    def landed(buf, send, recv, s):
        remote(buf.at[s], buf.at[s], send.at[0], recv.at[s], {"ctx": sibling}).wait_recv()

    def forward(buf, send, recv):
        for r in range(1, chips):
            s = chip_at(chips - r)
            landed(buf, send, recv, s)
            copy = remote(buf.at[s], buf.at[s], send.at[chips - 1 + r], recv.at[s], {"ctx": sibling})
            copy.start()
            pending.append(copy)

    def from_sibling(buf, send, recv):
        for r in range(chips):
            landed(buf, send, recv, lax.rem(chip + r, chips) * 2 + 1 - core)

    for i, ref in enumerate((key, value)):
        copy = remote(ref.at[0], kvbuf.at[i, core], kv_send.at[i], kv_recv.at[i], {"ctx": sibling})
        copy.start()
        pending.append(copy)

    def ask(r):
        return remote(
            query_in.at[0], queries_in.at[r], q_send.at[r], q_recv.at[r], {"ctx": chip_at(chips - r)}
        )

    def answer(r):
        where = {"ctx": chip_at(r)}
        return (
            remote(part_out.at[r], part_in.at[r], part_send.at[r], part_recv.at[r], where),
            remote(stat_out.at[r], stat_in.at[r], stat_send.at[r], stat_recv.at[r], where),
        )

    for r in range(1, chips):

        @pl.when(chip >= r)
        def _(r=r):
            ask(r).start()

    offsets = [0]
    for r in range(1, n_exp // 2 + 1):
        offsets.append(r)
        if n_exp - r != r:
            offsets.append(n_exp - r)
    own_half = out_proj.at[pl.ds(pl.multiple_of(core * half, half), half)]
    for r in reversed(offsets[1:]):
        copy = remote(own_half, proj.at[e, core], proj_send.at[r], proj_recv.at[e, core], {"exp": exp_at(r)})
        copy.start()
        pending.append(copy)

    gate_parts = [gate_up.at[0, pl.ds(i * part_depth, part_depth)] for i in range(2)]
    gate_views = [(gbuf.at[:, i], g_send.at[i], g_recv.at[i]) for i in range(2)]

    def proj_at(s, side):
        return remote(proj.at[s, side], proj.at[s, side], proj_fwd.at[s], proj_recv.at[s, side], {"ctx": sibling})

    for copy in locals_:
        copy.wait()

    eye = jnp.where(
        lax.broadcasted_iota(jnp.int32, (tok, tok), 1) == lax.broadcasted_iota(jnp.int32, (tok, tok), 0), 1.0, 0.0
    ).astype(jnp.bfloat16)
    ids = lax.dot_general(
        eye,
        ids_ref[...].astype(jnp.float32).astype(jnp.bfloat16),
        (((1,), (1,)), ((), ())),
        preferred_element_type=jnp.float32,
    ).astype(jnp.int32)
    slots = []
    for k in range(2):
        away = ids[:, k : k + 1] - e
        away = jnp.where(away < 0, away + n_exp, away)
        slot = jnp.where(2 * away <= n_exp, 2 * away - 1, 2 * (n_exp - away))
        slots.append(jnp.where(away == 0, 0, slot))
    lane = lax.broadcasted_iota(jnp.int32, (tok, 128), 1)
    picks = [lane == slots[k] for k in range(2)]
    member = jnp.where(picks[0] | picks[1], 1.0, 0.0)
    below = jnp.where(
        lax.broadcasted_iota(jnp.int32, (tok, tok), 1) < lax.broadcasted_iota(jnp.int32, (tok, tok), 0), 1.0, 0.0
    ).astype(jnp.bfloat16)
    rank = jnp.dot(below, member.astype(jnp.bfloat16), preferred_element_type=jnp.float32)
    place = (member * (rank + 1.0)).astype(jnp.bfloat16)
    grid = (n_exp, cap, 128)
    rows = n_exp * cap
    spread_out = jnp.where(
        lax.broadcasted_iota(jnp.int32, grid, 0) == lax.broadcasted_iota(jnp.int32, grid, 2), 1.0, 0.0
    ).reshape(rows, 128)
    wanted = (lax.broadcasted_iota(jnp.int32, (n_exp, cap, tok), 1) + 1).astype(jnp.float32).reshape(rows, tok)
    held = lax.dot_general(
        spread_out.astype(jnp.bfloat16), place, (((1,), (1,)), ((), ())), preferred_element_type=jnp.float32
    )
    dispatch[...] = jnp.where(held == wanted, 1.0, 0.0).astype(jnp.bfloat16)
    column = lax.broadcasted_iota(jnp.int32, (tok, rows), 1).astype(jnp.float32)
    for k in range(2):
        own_rank = jnp.sum(jnp.where(picks[k], rank, 0.0), axis=1, keepdims=True)
        target = slots[k].astype(jnp.float32) * cap + own_rank
        chosen[k] = jnp.where(column == target, 1.0, 0.0)

    for r in range(1, chips):

        @pl.when(chip >= r)
        def _(r=r):
            ask(r).wait_send()

    first_half = spread(gate_parts[0], *gate_views[0])
    for i in range(2):
        remote(kvbuf.at[i, 0], kvbuf.at[i, 0], kv_send.at[i], kv_recv.at[i], {"ctx": sibling}).wait_recv()

    keys = 2 * tok
    stat_lane = lax.broadcasted_iota(jnp.int32, (tok, 128), 1)
    allowed = lax.broadcasted_iota(jnp.int32, (tok, keys), 1) <= core * tok + lax.broadcasted_iota(
        jnp.int32, (tok, keys), 0
    )

    def attend(asked, mask, keep):
        stats = jnp.zeros((tok, 128), jnp.float32)
        for h in range(HEADS):
            cols = slice(h * HEAD_DIM, (h + 1) * HEAD_DIM)
            scores = lax.dot_general(
                asked(cols),
                kvbuf[0, :, :, cols].reshape(keys, HEAD_DIM),
                (((1,), (1,)), ((), ())),
                preferred_element_type=jnp.float32,
            ) * (HEAD_DIM**-0.5)
            if mask:
                scores = jnp.where(allowed, scores, NEG_FILL)
            top = jnp.max(scores, axis=1, keepdims=True)
            weights = jnp.exp(scores - top)
            total = jnp.sum(weights, axis=1, keepdims=True)
            part = jnp.dot(
                weights.astype(jnp.bfloat16),
                kvbuf[1, :, :, cols].reshape(keys, HEAD_DIM),
                preferred_element_type=jnp.float32,
            )
            keep(cols, part / total)
            stats = jnp.where(stat_lane == h, top, jnp.where(stat_lane == 64 + h, total, stats))
        return stats

    for r in range(1, chips):

        @pl.when(chip + r < chips)
        def _(r=r):
            ask(r).wait_recv()

            def keep(cols, part):
                part_out[r, :, cols] = part.astype(jnp.bfloat16)

            stat_out[r] = attend(lambda cols: queries_in[r, :, cols], False, keep)
            for copy in answer(r):
                copy.start()

        @pl.when(chip < r)
        def _(r=r):
            part_in[r] = jnp.zeros((tok, width), jnp.bfloat16)
            stat_in[r] = jnp.where(stat_lane < 64, NEG_FILL, 0.0)

    def keep_own(cols, part):
        own_part[:, cols] = part

    stat_out[0] = attend(lambda cols: query[:, cols], True, keep_own)
    for r in range(1, chips):

        @pl.when(chip + r < chips)
        def _(r=r):
            for copy in answer(r):
                copy.wait_send()

    pending.extend(spread(gate_parts[1], *gate_views[1]))
    for r in offsets[1:]:
        s = exp_at(r)
        proj_at(s, core).wait_recv()
        copy = proj_at(s, core)
        copy.start()
        pending.append(copy)
    for r in range(1, chips):

        @pl.when(chip >= r)
        def _(r=r):
            for copy in answer(r):
                copy.wait_recv()

    all_stats = [stat_out[0]] + [stat_in[r] for r in range(1, chips)]
    for h in range(HEADS):
        cols = slice(h * HEAD_DIM, (h + 1) * HEAD_DIM)
        tops = [stat[:, h : h + 1] for stat in all_stats]
        highest = functools.reduce(jnp.maximum, tops)
        shares = [jnp.exp(top - highest) * stat[:, 64 + h : 65 + h] for top, stat in zip(tops, all_stats)]
        summed = shares[0] * own_part[:, cols]
        for r in range(1, chips):
            summed = summed + shares[r] * part_in[r, :, cols].astype(jnp.float32)
        context[:, cols] = (summed / functools.reduce(jnp.add, shares)).astype(jnp.bfloat16)

    for r in offsets[1:]:
        proj_at(exp_at(r), 1 - core).wait_recv()
    attn_out = jnp.dot(
        context[...], proj[...].reshape(n_exp * 2 * half, width), preferred_element_type=jnp.float32
    )
    hidden = (residual[...].astype(jnp.float32) + attn_out).astype(jnp.bfloat16)
    hidden_part[...] = hidden
    wide = hidden.astype(jnp.float32)
    mean_square = jnp.mean(wide * wide, axis=1, keepdims=True)
    normed = (wide * lax.rsqrt(mean_square + 1e-06)).astype(jnp.bfloat16)

    group = n_exp // 2
    for first in (group, 0):
        sent = jnp.dot(
            dispatch[first * cap : (first + group) * cap], normed, preferred_element_type=jnp.float32
        ).astype(jnp.bfloat16)
        outgoing[first : first + group] = sent.reshape(group, cap, width)
        for i in reversed(range(max(first, 1), first + group)):
            copy = remote(
                outgoing.at[i], arrived.at[i], out_send.at[i], out_recv.at[i], {"exp": exp_at(offsets[i])}
            )
            copy.start()
            pending.append(copy)
    arrived[0] = outgoing[0]

    affinity = jax.nn.sigmoid(
        lax.dot_general(normed, router[...], (((1,), (1,)), ((), ())), preferred_element_type=jnp.float32)
    )
    expert_lane = lax.broadcasted_iota(jnp.int32, affinity.shape, 1)
    picked = [
        jnp.sum(jnp.where(expert_lane == ids[:, k : k + 1], affinity, 0.0), axis=1, keepdims=True) for k in range(2)
    ]
    both = picked[0] + picked[1]
    combine = jnp.zeros((tok, rows), jnp.float32)
    for k in range(2):
        combine = combine + chosen[k] * (picked[k] / both)
    combine_part[...] = combine.astype(jnp.bfloat16)
    results = [
        pltpu.make_async_copy(hidden_part, hidden_out, local_sem.at[9]),
        pltpu.make_async_copy(combine_part, combine_out, local_sem.at[10]),
    ]
    for copy in results:
        copy.start()

    for copy in first_half:
        copy.wait_send()
    forward(*gate_views[0])
    pending.extend(spread(down.at[0], dbuf, d_send, d_recv))
    forward(*gate_views[1])
    from_sibling(*gate_views[0])
    from_sibling(*gate_views[1])
    ff = activation.shape[1]
    chunk = 256
    for first in (0, group):
        if first == group:
            forward(dbuf, d_send, d_recv)
        for i in range(max(first, 1), first + group):
            remote(
                outgoing.at[i], arrived.at[i], out_send.at[i], out_recv.at[i], {"exp": exp_at(offsets[i])}
            ).wait_recv()
        feats = arrived[first : first + group].reshape(group * cap, width)
        for f in range(0, ff, chunk):
            gate = jnp.dot(
                feats, gbuf[:, :, :, f : f + chunk].reshape(width, chunk), preferred_element_type=jnp.float32
            )
            up = jnp.dot(
                feats, gbuf[:, :, :, ff + f : ff + f + chunk].reshape(width, chunk), preferred_element_type=jnp.float32
            )
            activation[first * cap : (first + group) * cap, f : f + chunk] = (
                gate / (1.0 + jnp.exp(-gate)) * up
            ).astype(jnp.bfloat16)
    from_sibling(dbuf, d_send, d_recv)
    for first in (group, 0):
        made = jnp.dot(
            activation[first * cap : (first + group) * cap],
            dbuf[...].reshape(ff, width),
            preferred_element_type=jnp.float32,
        )
        produced[first : first + group] = made.astype(jnp.bfloat16).reshape(group, cap, width)
        for i in reversed(range(max(first, 1), first + group)):
            copy = remote(
                produced.at[i],
                returned.at[i],
                back_send.at[i],
                back_recv.at[i],
                {"exp": exp_at(n_exp - offsets[i])},
            )
            copy.start()
            pending.append(copy)
    own = pltpu.make_async_copy(produced.at[0], returned.at[0], local_sem.at[11])
    own.start()
    results.append(own)
    for i in range(1, n_exp):
        remote(produced.at[i], returned.at[i], back_send.at[i], back_recv.at[i], {"exp": exp_at(offsets[i])}).wait_recv()
    for copy in results:
        copy.wait()
    for copy in pending:
        copy.wait_send()


def on_device(
    residual, query_rows, key_rows, value_rows, out_proj, router, expert_ids, expert_gate_up, expert_down
):
    n_ctx = lax.axis_size("ctx")
    n_exp = lax.axis_size("exp")
    chips = n_ctx // 2
    _, tok, width = residual.shape
    cap = min(tok, -(-(3 * tok // n_exp) // 16) * 16)
    bf16 = jnp.bfloat16
    depth, twice_ff = expert_gate_up.shape[1:]
    ff_part = expert_down.shape[1]
    half = out_proj.shape[0] // 2
    anywhere = pl.BlockSpec(memory_space=pl.ANY)
    dma = pltpu.SemaphoreType.DMA
    ctx_sems = [dma((2 * chips,)), dma((n_ctx,))]
    rows = n_exp * cap
    returned, hidden, combine = pl.pallas_call(
        functools.partial(fused, n_ctx, n_exp, cap),
        out_shape=[
            jax.ShapeDtypeStruct((n_exp, cap, width), bf16),
            jax.ShapeDtypeStruct((tok, width), bf16),
            jax.ShapeDtypeStruct((tok, rows), bf16),
        ],
        in_specs=[anywhere] * 9,
        out_specs=[anywhere] * 3,
        scratch_shapes=[
            pltpu.VMEM((tok, width), bf16),
            pltpu.VMEM((tok, width), bf16),
            pltpu.VMEM((n_exp, width), bf16),
            pltpu.VMEM((2, tok), jnp.int32),
            pltpu.VMEM((2, 2, tok, width), bf16),
            pltpu.VMEM((n_exp, 2, half, width), bf16),
            pltpu.VMEM((n_ctx, 2, depth // 2, twice_ff), bf16),
            pltpu.VMEM((n_ctx, ff_part, width), bf16),
            pltpu.VMEM((n_exp, cap, width), bf16),
            pltpu.VMEM((n_exp, cap, width), bf16),
            pltpu.VMEM((n_exp, cap, width), bf16),
            pltpu.VMEM((rows, tok), bf16),
            pltpu.VMEM((2, tok, rows), jnp.float32),
            pltpu.VMEM((tok, width), bf16),
            pltpu.VMEM((tok, rows), bf16),
            pltpu.VMEM((tok, width), bf16),
            pltpu.VMEM((rows, twice_ff // 2), bf16),
            dma((12,)),
            pltpu.VMEM((chips, tok, width), bf16),
            pltpu.VMEM((chips, tok, width), bf16),
            pltpu.VMEM((chips, tok, width), bf16),
            pltpu.VMEM((chips, tok, 128), jnp.float32),
            pltpu.VMEM((chips, tok, 128), jnp.float32),
            pltpu.VMEM((tok, width), jnp.float32),
            dma((2,)),
            dma((2,)),
            dma((2,)),
        ]
        + [dma((chips,))] * 6
        + [dma((2, 2 * chips)), dma((2, n_ctx))]
        + ctx_sems
        + [dma((n_exp,)), dma((n_exp, 2)), dma((n_exp,))]
        + [dma((n_exp,))] * 4,
        compiler_params=pltpu.CompilerParams(
            collective_id=0, has_side_effects=True, vmem_limit_bytes=60 * 1024 * 1024
        ),
    )(
        residual,
        query_rows,
        router.T,
        jnp.swapaxes(expert_ids, 1, 2),
        key_rows,
        value_rows,
        out_proj,
        expert_gate_up,
        expert_down,
    )
    moe = jnp.dot(combine, returned.reshape(rows, width), preferred_element_type=jnp.float32)
    return (hidden.astype(jnp.float32) + moe).astype(bf16)[None]


def solution(mesh):
    return jax.shard_map(
        on_device,
        mesh=mesh,
        in_specs=(
            P("exp", "ctx", None),
            P("exp", "ctx", None),
            P("exp", "ctx", None),
            P("exp", "ctx", None),
            P("exp", None),
            P(),
            P("exp", "ctx", None),
            P("exp", "ctx", None),
            P("exp", "ctx", None),
        ),
        out_specs=P("exp", "ctx", None),
        check_vma=False,
    )
```

```python
import functools

import jax
import jax.numpy as jnp
from jax import lax
from jax.experimental import pallas as pl
from jax.experimental.pallas import tpu as pltpu
from jax.sharding import PartitionSpec as P

HEADS = 8
HEAD_DIM = 128
NEG_FILL = -1e30
MESH = pl.DeviceIdType.MESH


def fused(
    n_ctx,
    n_exp,
    cap,
    residual_in,
    query_in,
    router_in,
    ids_in,
    key,
    value,
    out_proj,
    gate_up,
    down,
    returned,
    hidden_out,
    combine_out,
    residual,
    query,
    router,
    ids_ref,
    kvbuf,
    proj,
    gbuf,
    dbuf,
    outgoing,
    arrived,
    produced,
    dispatch,
    chosen,
    hidden_part,
    combine_part,
    context,
    activation,
    local_sem,
    queries_in,
    part_out,
    part_in,
    stat_out,
    stat_in,
    own_part,
    kv_local,
    kv_send,
    kv_recv,
    q_send,
    q_recv,
    part_send,
    part_recv,
    stat_send,
    stat_recv,
    g_send,
    g_recv,
    d_send,
    d_recv,
    proj_send,
    proj_recv,
    proj_fwd,
    out_send,
    out_recv,
    back_send,
    back_recv,
):
    chips = n_ctx // 2
    c = lax.axis_index("ctx")
    e = lax.axis_index("exp")
    chip = c // 2
    core = lax.rem(c, 2)
    sibling = chip * 2 + 1 - core
    tok, width = query.shape
    half = out_proj.shape[0] // 2
    part_depth = gbuf.shape[2]

    def chip_at(r):
        return lax.rem(chip + r, chips) * 2 + core

    def exp_at(r):
        return lax.rem(e + r, n_exp)

    barrier = pltpu.get_barrier_semaphore()
    for r in range(1, n_exp):
        pl.semaphore_signal(barrier, inc=1, device_id={"exp": exp_at(r)}, device_id_type=MESH)
    for r in range(1, chips):
        pl.semaphore_signal(barrier, inc=1, device_id={"ctx": chip_at(r)}, device_id_type=MESH)
    pl.semaphore_signal(barrier, inc=1, device_id={"ctx": sibling}, device_id_type=MESH)

    locals_ = [
        pltpu.make_async_copy(query_in.at[0], query, local_sem.at[0]),
        pltpu.make_async_copy(residual_in.at[0], residual, local_sem.at[1]),
        pltpu.make_async_copy(out_proj.at[pl.ds(0, half)], proj.at[e, 0], local_sem.at[2]),
        pltpu.make_async_copy(out_proj.at[pl.ds(half, half)], proj.at[e, 1], local_sem.at[3]),
        pltpu.make_async_copy(gate_up.at[0, pl.ds(0, part_depth)], gbuf.at[c, 0], local_sem.at[4]),
        pltpu.make_async_copy(gate_up.at[0, pl.ds(part_depth, part_depth)], gbuf.at[c, 1], local_sem.at[8]),
        pltpu.make_async_copy(down.at[0], dbuf.at[c], local_sem.at[5]),
        pltpu.make_async_copy(router_in, router, local_sem.at[6]),
        pltpu.make_async_copy(ids_in.at[0], ids_ref, local_sem.at[7]),
    ]
    for i, ref in enumerate((key, value)):
        locals_.append(pltpu.make_async_copy(ref.at[0], kvbuf.at[i, core], kv_local.at[i]))
    for copy in locals_:
        copy.start()
    pl.semaphore_wait(barrier, n_exp - 1 + chips - 1 + 1)

    pending = []

    def remote(src, dst, send, recv, where):
        return pltpu.make_async_remote_copy(
            src_ref=src, dst_ref=dst, send_sem=send, recv_sem=recv, device_id=where, device_id_type=MESH
        )

    def spread(src, buf, send, recv):
        copies = []
        for r in range(1, chips):
            copies.append(remote(src, buf.at[c], send.at[r - 1], recv.at[c], {"ctx": chip_at(r)}))
        copies.append(remote(src, buf.at[c], send.at[chips - 1], recv.at[c], {"ctx": sibling}))
        for copy in copies:
            copy.start()
        return copies

    def landed(buf, send, recv, s):
        remote(buf.at[s], buf.at[s], send.at[0], recv.at[s], {"ctx": sibling}).wait_recv()

    def forward(buf, send, recv):
        for r in range(1, chips):
            s = chip_at(chips - r)
            landed(buf, send, recv, s)
            copy = remote(buf.at[s], buf.at[s], send.at[chips - 1 + r], recv.at[s], {"ctx": sibling})
            copy.start()
            pending.append(copy)

    def from_sibling(buf, send, recv):
        for r in range(chips):
            landed(buf, send, recv, lax.rem(chip + r, chips) * 2 + 1 - core)

    for i, ref in enumerate((key, value)):
        copy = remote(ref.at[0], kvbuf.at[i, core], kv_send.at[i], kv_recv.at[i], {"ctx": sibling})
        copy.start()
        pending.append(copy)

    def ask(r):
        return remote(
            query_in.at[0], queries_in.at[r], q_send.at[r], q_recv.at[r], {"ctx": chip_at(chips - r)}
        )

    def answer(r):
        where = {"ctx": chip_at(r)}
        return (
            remote(part_out.at[r], part_in.at[r], part_send.at[r], part_recv.at[r], where),
            remote(stat_out.at[r], stat_in.at[r], stat_send.at[r], stat_recv.at[r], where),
        )

    for r in range(1, chips):

        @pl.when(chip >= r)
        def _(r=r):
            ask(r).start()

    offsets = [0]
    for r in range(1, n_exp // 2 + 1):
        offsets.append(r)
        if n_exp - r != r:
            offsets.append(n_exp - r)
    own_half = out_proj.at[pl.ds(pl.multiple_of(core * half, half), half)]
    for r in reversed(offsets[1:]):
        copy = remote(own_half, proj.at[e, core], proj_send.at[r], proj_recv.at[e, core], {"exp": exp_at(r)})
        copy.start()
        pending.append(copy)

    gate_parts = [gate_up.at[0, pl.ds(i * part_depth, part_depth)] for i in range(2)]
    gate_views = [(gbuf.at[:, i], g_send.at[i], g_recv.at[i]) for i in range(2)]

    def proj_at(s, side):
        return remote(proj.at[s, side], proj.at[s, side], proj_fwd.at[s], proj_recv.at[s, side], {"ctx": sibling})

    for copy in locals_:
        copy.wait()

    eye = jnp.where(
        lax.broadcasted_iota(jnp.int32, (tok, tok), 1) == lax.broadcasted_iota(jnp.int32, (tok, tok), 0), 1.0, 0.0
    ).astype(jnp.bfloat16)
    ids = lax.dot_general(
        eye,
        ids_ref[...].astype(jnp.float32).astype(jnp.bfloat16),
        (((1,), (1,)), ((), ())),
        preferred_element_type=jnp.float32,
    ).astype(jnp.int32)
    slots = []
    for k in range(2):
        away = ids[:, k : k + 1] - e
        away = jnp.where(away < 0, away + n_exp, away)
        slot = jnp.where(2 * away <= n_exp, 2 * away - 1, 2 * (n_exp - away))
        slots.append(jnp.where(away == 0, 0, slot))
    lane = lax.broadcasted_iota(jnp.int32, (tok, 128), 1)
    picks = [lane == slots[k] for k in range(2)]
    member = jnp.where(picks[0] | picks[1], 1.0, 0.0)
    below = jnp.where(
        lax.broadcasted_iota(jnp.int32, (tok, tok), 1) < lax.broadcasted_iota(jnp.int32, (tok, tok), 0), 1.0, 0.0
    ).astype(jnp.bfloat16)
    rank = jnp.dot(below, member.astype(jnp.bfloat16), preferred_element_type=jnp.float32)
    place = (member * (rank + 1.0)).astype(jnp.bfloat16)
    grid = (n_exp, cap, 128)
    rows = n_exp * cap
    spread_out = jnp.where(
        lax.broadcasted_iota(jnp.int32, grid, 0) == lax.broadcasted_iota(jnp.int32, grid, 2), 1.0, 0.0
    ).reshape(rows, 128)
    wanted = (lax.broadcasted_iota(jnp.int32, (n_exp, cap, tok), 1) + 1).astype(jnp.float32).reshape(rows, tok)
    held = lax.dot_general(
        spread_out.astype(jnp.bfloat16), place, (((1,), (1,)), ((), ())), preferred_element_type=jnp.float32
    )
    dispatch[...] = jnp.where(held == wanted, 1.0, 0.0).astype(jnp.bfloat16)
    column = lax.broadcasted_iota(jnp.int32, (tok, rows), 1).astype(jnp.float32)
    for k in range(2):
        own_rank = jnp.sum(jnp.where(picks[k], rank, 0.0), axis=1, keepdims=True)
        target = slots[k].astype(jnp.float32) * cap + own_rank
        chosen[k] = jnp.where(column == target, 1.0, 0.0)

    for r in range(1, chips):

        @pl.when(chip >= r)
        def _(r=r):
            ask(r).wait_send()

    first_half = spread(gate_parts[0], *gate_views[0])
    for i in range(2):
        remote(kvbuf.at[i, 0], kvbuf.at[i, 0], kv_send.at[i], kv_recv.at[i], {"ctx": sibling}).wait_recv()

    keys = 2 * tok
    stat_lane = lax.broadcasted_iota(jnp.int32, (tok, 128), 1)
    allowed = lax.broadcasted_iota(jnp.int32, (tok, keys), 1) <= core * tok + lax.broadcasted_iota(
        jnp.int32, (tok, keys), 0
    )

    def attend(asked, mask, keep):
        stats = jnp.zeros((tok, 128), jnp.float32)
        for h in range(HEADS):
            cols = slice(h * HEAD_DIM, (h + 1) * HEAD_DIM)
            scores = lax.dot_general(
                asked(cols),
                kvbuf[0, :, :, cols].reshape(keys, HEAD_DIM),
                (((1,), (1,)), ((), ())),
                preferred_element_type=jnp.float32,
            ) * (HEAD_DIM**-0.5)
            if mask:
                scores = jnp.where(allowed, scores, NEG_FILL)
            top = jnp.max(scores, axis=1, keepdims=True)
            weights = jnp.exp(scores - top)
            total = jnp.sum(weights, axis=1, keepdims=True)
            part = jnp.dot(
                weights.astype(jnp.bfloat16),
                kvbuf[1, :, :, cols].reshape(keys, HEAD_DIM),
                preferred_element_type=jnp.float32,
            )
            keep(cols, part / total)
            stats = jnp.where(stat_lane == h, top, jnp.where(stat_lane == 64 + h, total, stats))
        return stats

    for r in range(1, chips):

        @pl.when(chip + r < chips)
        def _(r=r):
            ask(r).wait_recv()

            def keep(cols, part):
                part_out[r, :, cols] = part.astype(jnp.bfloat16)

            stat_out[r] = attend(lambda cols: queries_in[r, :, cols], False, keep)
            for copy in answer(r):
                copy.start()

        @pl.when(chip < r)
        def _(r=r):
            part_in[r] = jnp.zeros((tok, width), jnp.bfloat16)
            stat_in[r] = jnp.where(stat_lane < 64, NEG_FILL, 0.0)

    def keep_own(cols, part):
        own_part[:, cols] = part

    stat_out[0] = attend(lambda cols: query[:, cols], True, keep_own)
    for r in range(1, chips):

        @pl.when(chip + r < chips)
        def _(r=r):
            for copy in answer(r):
                copy.wait_send()

    pending.extend(spread(gate_parts[1], *gate_views[1]))
    for r in offsets[1:]:
        s = exp_at(r)
        proj_at(s, core).wait_recv()
        copy = proj_at(s, core)
        copy.start()
        pending.append(copy)
    for r in range(1, chips):

        @pl.when(chip >= r)
        def _(r=r):
            for copy in answer(r):
                copy.wait_recv()

    all_stats = [stat_out[0]] + [stat_in[r] for r in range(1, chips)]
    for h in range(HEADS):
        cols = slice(h * HEAD_DIM, (h + 1) * HEAD_DIM)
        tops = [stat[:, h : h + 1] for stat in all_stats]
        highest = functools.reduce(jnp.maximum, tops)
        shares = [jnp.exp(top - highest) * stat[:, 64 + h : 65 + h] for top, stat in zip(tops, all_stats)]
        summed = shares[0] * own_part[:, cols]
        for r in range(1, chips):
            summed = summed + shares[r] * part_in[r, :, cols].astype(jnp.float32)
        context[:, cols] = (summed / functools.reduce(jnp.add, shares)).astype(jnp.bfloat16)

    for r in offsets[1:]:
        proj_at(exp_at(r), 1 - core).wait_recv()
    attn_out = jnp.dot(
        context[...], proj[...].reshape(n_exp * 2 * half, width), preferred_element_type=jnp.float32
    )
    hidden = (residual[...].astype(jnp.float32) + attn_out).astype(jnp.bfloat16)
    hidden_part[...] = hidden
    wide = hidden.astype(jnp.float32)
    mean_square = jnp.mean(wide * wide, axis=1, keepdims=True)
    normed = (wide * lax.rsqrt(mean_square + 1e-06)).astype(jnp.bfloat16)

    group = n_exp // 2
    for first in (group, 0):
        sent = jnp.dot(
            dispatch[first * cap : (first + group) * cap], normed, preferred_element_type=jnp.float32
        ).astype(jnp.bfloat16)
        outgoing[first : first + group] = sent.reshape(group, cap, width)
        for i in reversed(range(max(first, 1), first + group)):
            copy = remote(
                outgoing.at[i], arrived.at[i], out_send.at[i], out_recv.at[i], {"exp": exp_at(offsets[i])}
            )
            copy.start()
            pending.append(copy)
    arrived[0] = outgoing[0]

    affinity = jax.nn.sigmoid(
        lax.dot_general(normed, router[...], (((1,), (1,)), ((), ())), preferred_element_type=jnp.float32)
    )
    expert_lane = lax.broadcasted_iota(jnp.int32, affinity.shape, 1)
    picked = [
        jnp.sum(jnp.where(expert_lane == ids[:, k : k + 1], affinity, 0.0), axis=1, keepdims=True) for k in range(2)
    ]
    both = picked[0] + picked[1]
    combine = jnp.zeros((tok, rows), jnp.float32)
    for k in range(2):
        combine = combine + chosen[k] * (picked[k] / both)
    combine_part[...] = combine.astype(jnp.bfloat16)
    results = [
        pltpu.make_async_copy(hidden_part, hidden_out, local_sem.at[9]),
        pltpu.make_async_copy(combine_part, combine_out, local_sem.at[10]),
    ]
    for copy in results:
        copy.start()

    for copy in first_half:
        copy.wait_send()
    forward(*gate_views[0])
    pending.extend(spread(down.at[0], dbuf, d_send, d_recv))
    forward(*gate_views[1])
    from_sibling(*gate_views[0])
    from_sibling(*gate_views[1])
    ff = activation.shape[1]
    chunk = 256
    for first in (0, group):
        if first == group:
            forward(dbuf, d_send, d_recv)
        for i in range(max(first, 1), first + group):
            remote(
                outgoing.at[i], arrived.at[i], out_send.at[i], out_recv.at[i], {"exp": exp_at(offsets[i])}
            ).wait_recv()
        feats = arrived[first : first + group].reshape(group * cap, width)
        for f in range(0, ff, chunk):
            gate = jnp.dot(
                feats, gbuf[:, :, :, f : f + chunk].reshape(width, chunk), preferred_element_type=jnp.float32
            )
            up = jnp.dot(
                feats, gbuf[:, :, :, ff + f : ff + f + chunk].reshape(width, chunk), preferred_element_type=jnp.float32
            )
            activation[first * cap : (first + group) * cap, f : f + chunk] = (
                gate / (1.0 + jnp.exp(-gate)) * up
            ).astype(jnp.bfloat16)
    from_sibling(dbuf, d_send, d_recv)
    quarter = n_exp // 4
    for first in reversed(range(0, n_exp, quarter)):
        made = jnp.dot(
            activation[first * cap : (first + quarter) * cap],
            dbuf[...].reshape(ff, width),
            preferred_element_type=jnp.float32,
        )
        produced[first : first + quarter] = made.astype(jnp.bfloat16).reshape(quarter, cap, width)
        for i in reversed(range(max(first, 1), first + quarter)):
            copy = remote(
                produced.at[i],
                returned.at[i],
                back_send.at[i],
                back_recv.at[i],
                {"exp": exp_at(n_exp - offsets[i])},
            )
            copy.start()
            pending.append(copy)
    own = pltpu.make_async_copy(produced.at[0], returned.at[0], local_sem.at[11])
    own.start()
    results.append(own)
    for i in range(1, n_exp):
        remote(produced.at[i], returned.at[i], back_send.at[i], back_recv.at[i], {"exp": exp_at(offsets[i])}).wait_recv()
    for copy in results:
        copy.wait()
    for copy in pending:
        copy.wait_send()


def on_device(
    residual, query_rows, key_rows, value_rows, out_proj, router, expert_ids, expert_gate_up, expert_down
):
    n_ctx = lax.axis_size("ctx")
    n_exp = lax.axis_size("exp")
    chips = n_ctx // 2
    _, tok, width = residual.shape
    cap = min(tok, -(-(3 * tok // n_exp) // 16) * 16)
    bf16 = jnp.bfloat16
    depth, twice_ff = expert_gate_up.shape[1:]
    ff_part = expert_down.shape[1]
    half = out_proj.shape[0] // 2
    anywhere = pl.BlockSpec(memory_space=pl.ANY)
    dma = pltpu.SemaphoreType.DMA
    ctx_sems = [dma((2 * chips,)), dma((n_ctx,))]
    rows = n_exp * cap
    returned, hidden, combine = pl.pallas_call(
        functools.partial(fused, n_ctx, n_exp, cap),
        out_shape=[
            jax.ShapeDtypeStruct((n_exp, cap, width), bf16),
            jax.ShapeDtypeStruct((tok, width), bf16),
            jax.ShapeDtypeStruct((tok, rows), bf16),
        ],
        in_specs=[anywhere] * 9,
        out_specs=[anywhere] * 3,
        scratch_shapes=[
            pltpu.VMEM((tok, width), bf16),
            pltpu.VMEM((tok, width), bf16),
            pltpu.VMEM((n_exp, width), bf16),
            pltpu.VMEM((2, tok), jnp.int32),
            pltpu.VMEM((2, 2, tok, width), bf16),
            pltpu.VMEM((n_exp, 2, half, width), bf16),
            pltpu.VMEM((n_ctx, 2, depth // 2, twice_ff), bf16),
            pltpu.VMEM((n_ctx, ff_part, width), bf16),
            pltpu.VMEM((n_exp, cap, width), bf16),
            pltpu.VMEM((n_exp, cap, width), bf16),
            pltpu.VMEM((n_exp, cap, width), bf16),
            pltpu.VMEM((rows, tok), bf16),
            pltpu.VMEM((2, tok, rows), jnp.float32),
            pltpu.VMEM((tok, width), bf16),
            pltpu.VMEM((tok, rows), bf16),
            pltpu.VMEM((tok, width), bf16),
            pltpu.VMEM((rows, twice_ff // 2), bf16),
            dma((12,)),
            pltpu.VMEM((chips, tok, width), bf16),
            pltpu.VMEM((chips, tok, width), bf16),
            pltpu.VMEM((chips, tok, width), bf16),
            pltpu.VMEM((chips, tok, 128), jnp.float32),
            pltpu.VMEM((chips, tok, 128), jnp.float32),
            pltpu.VMEM((tok, width), jnp.float32),
            dma((2,)),
            dma((2,)),
            dma((2,)),
        ]
        + [dma((chips,))] * 6
        + [dma((2, 2 * chips)), dma((2, n_ctx))]
        + ctx_sems
        + [dma((n_exp,)), dma((n_exp, 2)), dma((n_exp,))]
        + [dma((n_exp,))] * 4,
        compiler_params=pltpu.CompilerParams(
            collective_id=0, has_side_effects=True, vmem_limit_bytes=60 * 1024 * 1024
        ),
    )(
        residual,
        query_rows,
        router.T,
        jnp.swapaxes(expert_ids, 1, 2),
        key_rows,
        value_rows,
        out_proj,
        expert_gate_up,
        expert_down,
    )
    moe = jnp.dot(combine, returned.reshape(rows, width), preferred_element_type=jnp.float32)
    return (hidden.astype(jnp.float32) + moe).astype(bf16)[None]


def solution(mesh):
    return jax.shard_map(
        on_device,
        mesh=mesh,
        in_specs=(
            P("exp", "ctx", None),
            P("exp", "ctx", None),
            P("exp", "ctx", None),
            P("exp", "ctx", None),
            P("exp", None),
            P(),
            P("exp", "ctx", None),
            P("exp", "ctx", None),
            P("exp", "ctx", None),
        ),
        out_specs=P("exp", "ctx", None),
        check_vma=False,
    )
```
